32 devices in a mesh: wide: 8 (over y, x, core), narrow: 4 (over z).
Axes of the slice: x: 2, y: 2, z: 4, core: 2. Of those that a mesh axis runs over, the one named last changes fastest.
Arguments:
- volume: bfloat16 [32, 32, 16, 128], P(None, 'wide', 'narrow'), may hold values from -6 to 6
- cotangent: bfloat16 [32, 32, 16, 128], P(None, 'wide', 'narrow'), may hold values from -6 to 6
- conv_first: bfloat16 [3, 3, 3, 32, 32], replicated, may hold values from -0.21875 to 0.21875
- conv_second: bfloat16 [3, 3, 3, 32, 64], replicated, may hold values from -0.21875 to 0.21875
- conv_bottom: bfloat16 [3, 3, 3, 64, 128], replicated, may hold values from -0.3125 to 0.3125
- lift_weight: bfloat16 [64, 128], replicated, may hold values from -2 to 2
- conv_decode: bfloat16 [3, 3, 3, 64, 32], replicated, may hold values from -0.15625 to 0.15625
- conv_final: bfloat16 [3, 3, 3, 32, 32], replicated, may hold values from -0.21875 to 0.21875
Outputs:
- features_out: bfloat16 [32, 32, 16, 128], P(None, 'wide', 'narrow')
- input_grad: bfloat16 [32, 32, 16, 128], P(None, 'wide', 'narrow')
The draws below stay inside these ranges and needn't reach their ends.
All inputs are finite; a program needn't handle non-finite values.
Results may differ from the reference program's by a relative error of at most 0.013.
Values may be sent and summed in bfloat16 or wider, within the bound.
A program may use at most 64 MiB of HBM per device.

```python
import jax
import jax.numpy as jnp
from jax import lax

C1 = 32
C2 = 64
C3 = 128
CZ = 128
NX = 32
NY = 16


def block_levels(own_key, dims, cuts, low, largest):
    gain, own = 1.0, jax.random.fold_in(own_key, 6)
    for position, parts in cuts:
        heights = jnp.exp(jax.random.uniform(jax.random.fold_in(own, position), (parts,), jnp.float32, low / len(cuts), largest / len(cuts)))
        gain = gain * jnp.repeat(heights, dims[position] // parts).reshape([-1 if axis == position else 1 for axis in range(len(dims))])
    return gain


def scatter_about(key, shape, width, most, shards=(), kind=jnp.bfloat16):
    entries = jax.random.normal(key, shape, jnp.float32) * width
    if len(shards) > 0:
        entries = block_levels(key, shape, shards, -0.22, 0.18) * entries
    return jnp.clip(entries, min=-most, max=most).astype(kind)


def setup_inputs(seed: int = 0) -> dict:
    keys = jax.random.split(jax.random.key(seed), 9)
    return {
        "volume": scatter_about(keys[0], (C1, NX, NY, CZ), 1.0, 6.0, ((1, 8), (2, 4))),
        "cotangent": scatter_about(keys[1], (C1, NX, NY, CZ), 1.0, 6.0, ((1, 8), (2, 4))),
        "conv_first": scatter_about(keys[2], (3, 3, 3, C1, C1), (27 * C1) ** -0.5, 0.21875),
        "conv_second": scatter_about(keys[3], (3, 3, 3, C1, C2), (27 * C1) ** -0.5, 0.21875),
        "conv_bottom": scatter_about(keys[4], (3, 3, 3, C2, C3), (27 * C2 // 4) ** -0.5, 0.3125),
        "lift_weight": scatter_about(keys[5], (C2, C3), (C3 // 16) ** -0.5, 2.0),
        "conv_decode": scatter_about(keys[6], (3, 3, 3, C2, C1), (27 * C2) ** -0.5, 0.15625),
        "conv_final": scatter_about(keys[7], (3, 3, 3, C1, C1), (27 * C1) ** -0.5, 0.21875),
    }


def conv(field, kernel):
    out = lax.conv_general_dilated(field.astype(jnp.float32)[None], kernel.astype(jnp.float32), (1, 1, 1), "SAME", dimension_numbers=("NCDHW", "DHWIO", "NCDHW"))
    return out[0]


def flipped(kernel):
    return jnp.flip(kernel, (0, 1, 2)).transpose(0, 1, 2, 4, 3)


def blocks(field):
    chans, xs, ys, zs = field.shape
    return field.astype(jnp.float32).reshape(chans, xs // 2, 2, ys // 2, 2, zs // 2, 2)


def pool_mean(field):
    return jnp.mean(blocks(field), axis=(2, 4, 6))


def pool_sum(field):
    return jnp.sum(blocks(field), axis=(2, 4, 6))


def upsample(field):
    return jnp.repeat(jnp.repeat(jnp.repeat(field, 2, 1), 2, 2), 2, 3)


def silu(value):
    return value * jax.nn.sigmoid(value)


def slope(value):
    sig = jax.nn.sigmoid(value)
    return sig * (1.0 + value * (1.0 - sig))


def pointwise(matrix, field):
    chans, xs, ys, zs = field.shape
    flat = field.astype(jnp.float32).reshape(chans, xs * ys * zs)
    out = jnp.dot(matrix.astype(jnp.float32), flat)
    return out.reshape(matrix.shape[0], xs, ys, zs)


def reference(volume, cotangent, conv_first, conv_second, conv_bottom, lift_weight, conv_decode, conv_final):
    bf = jnp.bfloat16
    f32 = jnp.float32
    pre_first = conv(volume, conv_first)
    hidden_first = silu(pre_first).astype(bf)
    pooled_first = pool_mean(hidden_first).astype(bf)
    pre_second = conv(pooled_first, conv_second)
    hidden_second = silu(pre_second).astype(bf)
    pooled_second = pool_mean(hidden_second).astype(bf)
    pre_bottom = conv(pooled_second, conv_bottom)
    hidden_bottom = silu(pre_bottom).astype(bf)
    joined_second = (upsample(pointwise(lift_weight, hidden_bottom)) + hidden_second.astype(f32)).astype(bf)
    pre_decode = conv(joined_second, conv_decode)
    hidden_decode = silu(pre_decode).astype(bf)
    joined_first = (upsample(hidden_decode.astype(f32)) + hidden_first.astype(f32)).astype(bf)
    features_out = conv(joined_first, conv_final).astype(bf)
    grad_joined = conv(cotangent, flipped(conv_final)).astype(bf)
    grad_decode = (pool_sum(grad_joined) * slope(pre_decode)).astype(bf)
    grad_second_up = conv(grad_decode, flipped(conv_decode)).astype(bf)
    grad_lift = pool_sum(grad_second_up).astype(bf)
    grad_bottom = (pointwise(lift_weight.T, grad_lift) * slope(pre_bottom)).astype(bf)
    grad_pool_second = conv(grad_bottom, flipped(conv_bottom))
    grad_second = ((grad_second_up.astype(f32) + upsample(grad_pool_second) / 8.0) * slope(pre_second)).astype(bf)
    grad_pool_first = conv(grad_second, flipped(conv_second))
    grad_first = ((grad_joined.astype(f32) + upsample(grad_pool_first) / 8.0) * slope(pre_first)).astype(bf)
    input_grad = conv(grad_first, flipped(conv_first)).astype(bf)
    return features_out, input_grad
```

```python
import functools

import jax
import jax.numpy as jnp
from jax import lax
from jax.experimental import pallas as pl
from jax.experimental.pallas import tpu as pltpu
from jax.sharding import PartitionSpec as P

BF = jnp.bfloat16
F32 = jnp.float32
SIDES = tuple((dx, dy) for dx in (-1, 0, 1) for dy in (-1, 0, 1) if (dx, dy) != (0, 0))


def sigmoid(value):
    return jax.nn.sigmoid(value)


def silu(value):
    return value * sigmoid(value)


def slope(value):
    sigma = sigmoid(value)
    return sigma * (1.0 + value * (1.0 - sigma))


def lane_of(value):
    return lax.broadcasted_iota(jnp.int32, value.shape, value.ndim - 1)


def conv(weights, edged, xs, step):
    lanes = edged.shape[2]
    depth = 3 * edged.shape[1]
    rows = weights.shape[0] // 3
    matrix = weights[...]
    outs = []
    for x in range(xs):
        part = jnp.dot(
            matrix, edged[x : x + 3].reshape(depth, lanes), preferred_element_type=F32
        )
        low, mid, high = part[:rows], part[rows : 2 * rows], part[2 * rows :]
        lane = lane_of(low)
        low = jnp.where(lane < step, 0.0, pltpu.roll(low, step, 1))
        high = jnp.where(lane >= lanes - step, 0.0, pltpu.roll(high, lanes - step, 1))
        outs.append(low + mid + high)
    return outs


def block_sum(fields, chans, step):
    outs = []
    for x in range(0, len(fields), 2):
        both = fields[x] + fields[x + 1]
        rows, lanes = both.shape
        both = jnp.concatenate(
            [
                both[y * chans : (y + 1) * chans] + both[(y + 1) * chans : (y + 2) * chans]
                for y in range(0, rows // chans, 2)
            ],
            axis=0,
        )
        lane = lane_of(both)
        other = jnp.where(
            lax.rem(lane // step, 2) == 0,
            pltpu.roll(both, lanes - step, 1),
            pltpu.roll(both, step, 1),
        )
        outs.append(both + other)
    return outs


def spread(fields, chans):
    outs = []
    for field in fields:
        parts = []
        for y in range(field.shape[0] // chans):
            cell = field[y * chans : (y + 1) * chans]
            parts += [cell, cell]
        wide = jnp.concatenate(parts, axis=0)
        outs += [wide, wide]
    return outs


def body(
    wide_count, narrow_count, xs, ys, chans,
    vol, cot, w_first, w_second, w_bottom, lift, lift_t, w_decode, w_final,
    b_first, b_second, b_bottom, b_decode, b_final,
    features_ref, grad_ref,
    e_vol, e_cot, e_p1, e_p2, e_j2, e_j1, e_gd, e_gb, e_gs, e_gf,
    pre_first, hidden_first, grad_joined, pre_second, hidden_second,
    send_sem, recv_sem,
):
    c1, c2, c3 = chans
    x2, y2 = xs // 2, ys // 2
    x3, y3 = x2 // 2, y2 // 2
    me_wide = lax.axis_index("wide")
    me_narrow = lax.axis_index("narrow")

    def exists(dx, dy):
        near_x, near_y = me_wide + dx, me_narrow + dy
        return (
            (near_x >= 0) & (near_x < wide_count) & (near_y >= 0) & (near_y < narrow_count)
        )

    def span(delta, count, sending):
        if delta == 0:
            return 1, count
        if sending:
            return (count if delta > 0 else 1), 1
        return (0 if delta > 0 else count + 1), 1

    def copy_of(index, edged, side, nx, ny, width):
        dx, dy = SIDES[side]

        def part(sending):
            x_at, x_len = span(dx, nx, sending)
            y_at, y_len = span(dy, ny, sending)
            return edged.at[pl.ds(x_at, x_len), pl.ds(y_at * width, y_len * width), :]

        return pltpu.make_async_remote_copy(
            src_ref=part(True),
            dst_ref=part(False),
            send_sem=send_sem.at[index, side],
            recv_sem=recv_sem.at[index, side],
            device_id=(me_wide + dx, me_narrow + dy),
            device_id_type=pl.DeviceIdType.MESH,
        )

    started = []

    def send(index, edged, nx, ny, width):
        for side, (dx, dy) in enumerate(SIDES):
            copy = copy_of(index, edged, side, nx, ny, width)
            pl.when(exists(dx, dy))(copy.start)
        started.append((index, edged, nx, ny, width))

    def receive(index, edged, nx, ny, width):
        for side, (dx, dy) in enumerate(SIDES):
            copy = copy_of(index, edged, side, nx, ny, width)
            pl.when(exists(-dx, -dy))(copy.wait_recv)

    def put(edged, fields, width):
        rows = fields[0].shape[0]
        for x, field in enumerate(fields):
            edged[x + 1, width : width + rows, :] = field.astype(BF)

    def clear(edged, nx, ny, width):
        lanes = edged.shape[2]
        edged[0] = jnp.zeros(((ny + 2) * width, lanes), BF)
        edged[nx + 1] = jnp.zeros(((ny + 2) * width, lanes), BF)
        for x in range(1, nx + 1):
            edged[x, 0:width, :] = jnp.zeros((width, lanes), BF)
            edged[x, (ny + 1) * width : (ny + 2) * width, :] = jnp.zeros((width, lanes), BF)

    spec_vol = (0, e_vol, xs, ys, c1)
    spec_cot = (1, e_cot, xs, ys, c1)
    spec_p1 = (2, e_p1, x2, y2, c1)
    spec_p2 = (3, e_p2, x3, y3, c2)
    spec_j2 = (4, e_j2, x2, y2, c2)
    spec_j1 = (5, e_j1, xs, ys, c1)
    spec_gd = (6, e_gd, x2, y2, c1)
    spec_gb = (7, e_gb, x3, y3, c3)
    spec_gs = (8, e_gs, x2, y2, c2)
    spec_gf = (9, e_gf, xs, ys, c1)
    for spec in (
        spec_vol, spec_cot, spec_p1, spec_p2, spec_j2, spec_j1, spec_gd, spec_gb, spec_gs, spec_gf
    ):
        clear(*spec[1:])

    barrier = pltpu.get_barrier_semaphore()
    for dx, dy in SIDES:

        @pl.when(exists(dx, dy))
        def _(dx=dx, dy=dy):
            pl.semaphore_signal(
                barrier,
                inc=1,
                device_id=(me_wide + dx, me_narrow + dy),
                device_id_type=pl.DeviceIdType.MESH,
            )

    put(e_vol, [vol[x] for x in range(xs)], c1)
    put(e_cot, [cot[x] for x in range(xs)], c1)
    across = 1 + (me_wide > 0).astype(jnp.int32) + (me_wide < wide_count - 1).astype(jnp.int32)
    along = 1 + (me_narrow > 0).astype(jnp.int32) + (me_narrow < narrow_count - 1).astype(jnp.int32)
    pl.semaphore_wait(barrier, across * along - 1)

    send(*spec_vol)
    send(*spec_cot)

    receive(*spec_vol)
    hidden = []
    for x, pre in enumerate(conv(w_first, e_vol, xs, 1)):
        pre_first[x] = pre
        hidden.append(silu(pre).astype(BF))
        hidden_first[x] = hidden[-1]
    pooled = block_sum([h.astype(F32) for h in hidden], c1, 1)
    put(e_p1, [p * 0.125 for p in pooled], c1)
    send(*spec_p1)

    receive(*spec_cot)
    joined = [g.astype(BF) for g in conv(b_final, e_cot, xs, 1)]
    for x in range(xs):
        grad_joined[x] = joined[x]
    joined_sum = block_sum([g.astype(F32) for g in joined], c1, 1)

    receive(*spec_p1)
    hidden = []
    for x, pre in enumerate(conv(w_second, e_p1, x2, 2)):
        pre_second[x] = pre
        hidden.append(silu(pre).astype(BF))
        hidden_second[x] = hidden[-1]
    pooled = block_sum([h.astype(F32) for h in hidden], c2, 2)
    put(e_p2, [p * 0.125 for p in pooled], c2)
    send(*spec_p2)

    receive(*spec_p2)
    pre_bottom = conv(w_bottom, e_p2, x3, 4)
    lifted = []
    for pre in pre_bottom:
        hid = silu(pre).astype(BF)
        lifted.append(
            jnp.concatenate(
                [
                    jnp.dot(lift[...], hid[y * c3 : (y + 1) * c3], preferred_element_type=F32)
                    for y in range(y3)
                ],
                axis=0,
            )
        )
    lifted = spread(lifted, c2)
    put(e_j2, [lifted[x] + hidden_second[x].astype(F32) for x in range(x2)], c2)
    send(*spec_j2)

    receive(*spec_j2)
    pre_decode = conv(w_decode, e_j2, x2, 2)
    put(e_gd, [joined_sum[x] * slope(pre_decode[x]) for x in range(x2)], c1)
    send(*spec_gd)
    decoded = spread([silu(pre).astype(BF).astype(F32) for pre in pre_decode], c1)
    put(e_j1, [decoded[x] + hidden_first[x].astype(F32) for x in range(xs)], c1)
    send(*spec_j1)

    receive(*spec_gd)
    second_up = [g.astype(BF).astype(F32) for g in conv(b_decode, e_gd, x2, 2)]
    grad_lift = [g.astype(BF) for g in block_sum(second_up, c2, 2)]
    grad_bottom = []
    for x in range(x3):
        back = jnp.concatenate(
            [
                jnp.dot(
                    lift_t[...],
                    grad_lift[x][y * c2 : (y + 1) * c2],
                    preferred_element_type=F32,
                )
                for y in range(y3)
            ],
            axis=0,
        )
        grad_bottom.append(back * slope(pre_bottom[x]))
    put(e_gb, grad_bottom, c3)
    send(*spec_gb)

    receive(*spec_j1)
    for x, out in enumerate(conv(w_final, e_j1, xs, 1)):
        features_ref[x] = out.astype(BF)

    receive(*spec_gb)
    pool_second = spread(conv(b_bottom, e_gb, x3, 4), c2)
    put(
        e_gs,
        [(second_up[x] + pool_second[x] * 0.125) * slope(pre_second[x]) for x in range(x2)],
        c2,
    )
    send(*spec_gs)

    receive(*spec_gs)
    pool_first = spread(conv(b_second, e_gs, x2, 2), c1)
    put(
        e_gf,
        [
            (grad_joined[x].astype(F32) + pool_first[x] * 0.125) * slope(pre_first[x])
            for x in range(xs)
        ],
        c1,
    )
    send(*spec_gf)

    receive(*spec_gf)
    for x, out in enumerate(conv(b_first, e_gf, xs, 1)):
        grad_ref[x] = out.astype(BF)

    for index, edged, nx, ny, width in started:
        for side, (dx, dy) in enumerate(SIDES):
            copy = copy_of(index, edged, side, nx, ny, width)
            pl.when(exists(dx, dy))(copy.wait_send)


def flipped(kernel):
    return jnp.flip(kernel, (0, 1, 2)).transpose(0, 1, 2, 4, 3)


def banded(kernel, ys):
    outs, ins = kernel.shape[4], kernel.shape[3]
    turned = kernel.transpose(2, 4, 0, 1, 3)
    stacked = jnp.stack(
        [
            jnp.pad(turned, ((0, 0), (0, 0), (0, 0), (y, ys - 1 - y), (0, 0)))
            for y in range(ys)
        ],
        axis=1,
    )
    return stacked.reshape(3 * ys * outs, 3 * (ys + 2) * ins)


def shards(
    wide_count, narrow_count,
    volume, cotangent, conv_first, conv_second, conv_bottom, lift_weight, conv_decode, conv_final
):
    c1, xs, ys, lanes = volume.shape
    c2, c3 = lift_weight.shape
    x2, y2, x3, y3 = xs // 2, ys // 2, xs // 4, ys // 4

    def columns(field):
        return field.transpose(1, 2, 0, 3).reshape(xs, ys * c1, lanes)

    def back(field):
        return field.reshape(xs, ys, c1, lanes).transpose(2, 0, 1, 3)

    def edged(nx, ny, width):
        return pltpu.VMEM((nx + 2, (ny + 2) * width, lanes), BF)

    shape = jax.ShapeDtypeStruct((xs, ys * c1, lanes), BF)
    vmem = pl.BlockSpec(memory_space=pltpu.VMEM)
    call = pl.pallas_call(
        functools.partial(body, wide_count, narrow_count, xs, ys, (c1, c2, c3)),
        out_shape=(shape, shape),
        in_specs=[vmem] * 14,
        out_specs=(vmem, vmem),
        scratch_shapes=[
            edged(xs, ys, c1),
            edged(xs, ys, c1),
            edged(x2, y2, c1),
            edged(x3, y3, c2),
            edged(x2, y2, c2),
            edged(xs, ys, c1),
            edged(x2, y2, c1),
            edged(x3, y3, c3),
            edged(x2, y2, c2),
            edged(xs, ys, c1),
            pltpu.VMEM((xs, ys * c1, lanes), F32),
            pltpu.VMEM((xs, ys * c1, lanes), BF),
            pltpu.VMEM((xs, ys * c1, lanes), BF),
            pltpu.VMEM((x2, y2 * c2, lanes), F32),
            pltpu.VMEM((x2, y2 * c2, lanes), BF),
            pltpu.SemaphoreType.DMA((10, 8)),
            pltpu.SemaphoreType.DMA((10, 8)),
        ],
        compiler_params=pltpu.CompilerParams(
            collective_id=0, has_side_effects=True, vmem_limit_bytes=40 * 1024 * 1024
        ),
    )
    features, grad = call(
        columns(volume),
        columns(cotangent),
        banded(conv_first, ys),
        banded(conv_second, y2),
        banded(conv_bottom, y3),
        lift_weight,
        lift_weight.T,
        banded(conv_decode, y2),
        banded(conv_final, ys),
        banded(flipped(conv_first), ys),
        banded(flipped(conv_second), y2),
        banded(flipped(conv_bottom), y3),
        banded(flipped(conv_decode), y2),
        banded(flipped(conv_final), ys),
    )
    return back(features), back(grad)


def solution(mesh):
    cells = P(None, "wide", "narrow", None)
    return jax.shard_map(
        functools.partial(shards, mesh.shape["wide"], mesh.shape["narrow"]),
        mesh=mesh,
        in_specs=(cells, cells, P(), P(), P(), P(), P(), P()),
        out_specs=(cells, cells),
        check_vma=False,
    )
```

```python
import functools

import jax
import jax.numpy as jnp
from jax import lax
from jax.experimental import pallas as pl
from jax.experimental.pallas import tpu as pltpu
from jax.sharding import PartitionSpec as P

BF = jnp.bfloat16
F32 = jnp.float32
SIDES = tuple((dx, dy) for dx in (-1, 0, 1) for dy in (-1, 0, 1) if (dx, dy) != (0, 0))


def sigmoid(value):
    return jax.nn.sigmoid(value)


def silu(value):
    return value * sigmoid(value)


def slope(value):
    sigma = sigmoid(value)
    return sigma * (1.0 + value * (1.0 - sigma))


def lane_of(value):
    return lax.broadcasted_iota(jnp.int32, value.shape, value.ndim - 1)


def conv(weights, edged, xs, step):
    lanes = edged.shape[2]
    depth = 3 * edged.shape[1]
    rows = weights.shape[0] // 3
    matrix = weights[...]
    outs = []
    for x in range(xs):
        part = jnp.dot(
            matrix, edged[x : x + 3].reshape(depth, lanes), preferred_element_type=F32
        )
        low, mid, high = part[:rows], part[rows : 2 * rows], part[2 * rows :]
        lane = lane_of(low)
        low = jnp.where(lane < step, 0.0, pltpu.roll(low, step, 1))
        high = jnp.where(lane >= lanes - step, 0.0, pltpu.roll(high, lanes - step, 1))
        outs.append(low + mid + high)
    return outs


def block_sum(fields, chans, step):
    outs = []
    for x in range(0, len(fields), 2):
        both = fields[x] + fields[x + 1]
        rows, lanes = both.shape
        both = jnp.concatenate(
            [
                both[y * chans : (y + 1) * chans] + both[(y + 1) * chans : (y + 2) * chans]
                for y in range(0, rows // chans, 2)
            ],
            axis=0,
        )
        lane = lane_of(both)
        other = jnp.where(
            lax.rem(lane // step, 2) == 0,
            pltpu.roll(both, lanes - step, 1),
            pltpu.roll(both, step, 1),
        )
        outs.append(both + other)
    return outs


def spread(fields, chans):
    outs = []
    for field in fields:
        parts = []
        for y in range(field.shape[0] // chans):
            cell = field[y * chans : (y + 1) * chans]
            parts += [cell, cell]
        wide = jnp.concatenate(parts, axis=0)
        outs += [wide, wide]
    return outs


def body(
    wide_count, narrow_count, xs, ys, chans,
    vol, cot, w_first, w_second, w_bottom, lift, w_decode, w_final,
    b_first, b_second, b_bottom, b_decode, b_final,
    features_ref, grad_ref,
    e_vol, e_cot, e_p1, e_p2, e_j2, e_j1, e_gd, e_gb, e_gs, e_gf,
    pre_first, hidden_first, grad_joined, pre_second, hidden_second,
    send_sem, recv_sem,
):
    c1, c2, c3 = chans
    x2, y2 = xs // 2, ys // 2
    x3, y3 = x2 // 2, y2 // 2
    me_wide = lax.axis_index("wide")
    me_narrow = lax.axis_index("narrow")

    def exists(dx, dy):
        near_x, near_y = me_wide + dx, me_narrow + dy
        return (
            (near_x >= 0) & (near_x < wide_count) & (near_y >= 0) & (near_y < narrow_count)
        )

    def span(delta, count, sending):
        if delta == 0:
            return 1, count
        if sending:
            return (count if delta > 0 else 1), 1
        return (0 if delta > 0 else count + 1), 1

    def copy_of(index, edged, side, nx, ny, width):
        dx, dy = SIDES[side]

        def part(sending):
            x_at, x_len = span(dx, nx, sending)
            y_at, y_len = span(dy, ny, sending)
            return edged.at[pl.ds(x_at, x_len), pl.ds(y_at * width, y_len * width), :]

        return pltpu.make_async_remote_copy(
            src_ref=part(True),
            dst_ref=part(False),
            send_sem=send_sem.at[index, side],
            recv_sem=recv_sem.at[index, side],
            device_id=(me_wide + dx, me_narrow + dy),
            device_id_type=pl.DeviceIdType.MESH,
        )

    started = []

    def send(index, edged, nx, ny, width):
        for side, (dx, dy) in enumerate(SIDES):
            copy = copy_of(index, edged, side, nx, ny, width)
            pl.when(exists(dx, dy))(copy.start)
        started.append((index, edged, nx, ny, width))

    def receive(index, edged, nx, ny, width):
        for side, (dx, dy) in enumerate(SIDES):
            copy = copy_of(index, edged, side, nx, ny, width)
            pl.when(exists(-dx, -dy))(copy.wait_recv)

    def put(edged, fields, width):
        rows = fields[0].shape[0]
        for x, field in enumerate(fields):
            edged[x + 1, width : width + rows, :] = field.astype(BF)

    def clear(edged, nx, ny, width):
        lanes = edged.shape[2]
        edged[0] = jnp.zeros(((ny + 2) * width, lanes), BF)
        edged[nx + 1] = jnp.zeros(((ny + 2) * width, lanes), BF)
        for x in range(1, nx + 1):
            edged[x, 0:width, :] = jnp.zeros((width, lanes), BF)
            edged[x, (ny + 1) * width : (ny + 2) * width, :] = jnp.zeros((width, lanes), BF)

    spec_vol = (0, e_vol, xs, ys, c1)
    spec_cot = (1, e_cot, xs, ys, c1)
    spec_p1 = (2, e_p1, x2, y2, c1)
    spec_p2 = (3, e_p2, x3, y3, c2)
    spec_j2 = (4, e_j2, x2, y2, c2)
    spec_j1 = (5, e_j1, xs, ys, c1)
    spec_gd = (6, e_gd, x2, y2, c1)
    spec_gb = (7, e_gb, x3, y3, c3)
    spec_gs = (8, e_gs, x2, y2, c2)
    spec_gf = (9, e_gf, xs, ys, c1)
    for spec in (
        spec_vol, spec_cot, spec_p1, spec_p2, spec_j2, spec_j1, spec_gd, spec_gb, spec_gs, spec_gf
    ):
        clear(*spec[1:])

    barrier = pltpu.get_barrier_semaphore()
    for dx, dy in SIDES:

        @pl.when(exists(dx, dy))
        def _(dx=dx, dy=dy):
            pl.semaphore_signal(
                barrier,
                inc=1,
                device_id=(me_wide + dx, me_narrow + dy),
                device_id_type=pl.DeviceIdType.MESH,
            )

    put(e_vol, [vol[x] for x in range(xs)], c1)
    put(e_cot, [cot[x] for x in range(xs)], c1)
    across = 1 + (me_wide > 0).astype(jnp.int32) + (me_wide < wide_count - 1).astype(jnp.int32)
    along = 1 + (me_narrow > 0).astype(jnp.int32) + (me_narrow < narrow_count - 1).astype(jnp.int32)
    pl.semaphore_wait(barrier, across * along - 1)

    send(*spec_vol)
    send(*spec_cot)

    receive(*spec_vol)
    hidden = []
    for x, pre in enumerate(conv(w_first, e_vol, xs, 1)):
        pre_first[x] = pre
        hidden.append(silu(pre).astype(BF))
        hidden_first[x] = hidden[-1]
    pooled = block_sum([h.astype(F32) for h in hidden], c1, 1)
    put(e_p1, [p * 0.125 for p in pooled], c1)
    send(*spec_p1)

    receive(*spec_cot)
    joined = [g.astype(BF) for g in conv(b_final, e_cot, xs, 1)]
    for x in range(xs):
        grad_joined[x] = joined[x]
    joined_sum = block_sum([g.astype(F32) for g in joined], c1, 1)

    receive(*spec_p1)
    hidden = []
    for x, pre in enumerate(conv(w_second, e_p1, x2, 2)):
        pre_second[x] = pre
        hidden.append(silu(pre).astype(BF))
        hidden_second[x] = hidden[-1]
    pooled = block_sum([h.astype(F32) for h in hidden], c2, 2)
    put(e_p2, [p * 0.125 for p in pooled], c2)
    send(*spec_p2)

    receive(*spec_p2)
    pre_bottom = conv(w_bottom, e_p2, x3, 4)
    lifted = []
    for pre in pre_bottom:
        hid = silu(pre).astype(BF)
        lifted.append(
            jnp.concatenate(
                [
                    jnp.dot(lift[...], hid[y * c3 : (y + 1) * c3], preferred_element_type=F32)
                    for y in range(y3)
                ],
                axis=0,
            )
        )
    lifted = spread(lifted, c2)
    put(e_j2, [lifted[x] + hidden_second[x].astype(F32) for x in range(x2)], c2)
    send(*spec_j2)

    receive(*spec_j2)
    pre_decode = conv(w_decode, e_j2, x2, 2)
    put(e_gd, [joined_sum[x] * slope(pre_decode[x]) for x in range(x2)], c1)
    send(*spec_gd)
    decoded = spread([silu(pre).astype(BF).astype(F32) for pre in pre_decode], c1)
    put(e_j1, [decoded[x] + hidden_first[x].astype(F32) for x in range(xs)], c1)
    send(*spec_j1)

    receive(*spec_gd)
    second_up = [g.astype(BF).astype(F32) for g in conv(b_decode, e_gd, x2, 2)]
    grad_lift = [g.astype(BF) for g in block_sum(second_up, c2, 2)]
    grad_bottom = []
    for x in range(x3):
        back = jnp.concatenate(
            [
                lax.dot_general(
                    lift[...],
                    grad_lift[x][y * c2 : (y + 1) * c2],
                    (((0,), (0,)), ((), ())),
                    preferred_element_type=F32,
                )
                for y in range(y3)
            ],
            axis=0,
        )
        grad_bottom.append(back * slope(pre_bottom[x]))
    put(e_gb, grad_bottom, c3)
    send(*spec_gb)

    receive(*spec_j1)
    for x, out in enumerate(conv(w_final, e_j1, xs, 1)):
        features_ref[x] = out.astype(BF)

    receive(*spec_gb)
    pool_second = spread(conv(b_bottom, e_gb, x3, 4), c2)
    put(
        e_gs,
        [(second_up[x] + pool_second[x] * 0.125) * slope(pre_second[x]) for x in range(x2)],
        c2,
    )
    send(*spec_gs)

    receive(*spec_gs)
    pool_first = spread(conv(b_second, e_gs, x2, 2), c1)
    put(
        e_gf,
        [
            (grad_joined[x].astype(F32) + pool_first[x] * 0.125) * slope(pre_first[x])
            for x in range(xs)
        ],
        c1,
    )
    send(*spec_gf)

    receive(*spec_gf)
    for x, out in enumerate(conv(b_first, e_gf, xs, 1)):
        grad_ref[x] = out.astype(BF)

    for index, edged, nx, ny, width in started:
        for side, (dx, dy) in enumerate(SIDES):
            copy = copy_of(index, edged, side, nx, ny, width)
            pl.when(exists(dx, dy))(copy.wait_send)


def forward_matrix(kernel, ys, ins, outs):
    zero = jnp.zeros((ins, outs), BF)
    strips = []
    for ex in range(3):
        for rim in range(ys + 2):
            strips.append(
                jnp.concatenate(
                    [
                        kernel[pl.ds(((ex * 3 + rim - y) * 3 + ez) * ins, ins), :]
                        if 0 <= rim - y < 3
                        else zero
                        for ez in range(3)
                        for y in range(ys)
                    ],
                    axis=1,
                )
            )
    turned = jnp.concatenate(strips, axis=0)
    size = 3 * ys * outs
    row = lax.broadcasted_iota(jnp.int32, (size, size), 0)
    column = lax.broadcasted_iota(jnp.int32, (size, size), 1)
    eye = jnp.where(row == column, 1.0, 0.0).astype(BF)
    return lax.dot_general(
        eye, turned, (((1,), (1,)), ((), ())), preferred_element_type=F32
    ).astype(BF)


def backward_strips(kernel, ys, outs, ins):
    zero = jnp.zeros((outs, ins), BF)
    return [
        jnp.concatenate(
            [
                kernel[pl.ds((((2 - ex) * 3 + 2 - rim + y) * 3 + 2 - ez) * outs, outs), :]
                if 0 <= rim - y < 3
                else zero
                for ex in range(3)
                for rim in range(ys + 2)
            ],
            axis=1,
        )
        for ez in range(3)
        for y in range(ys)
    ]


def prepare(
    xs, ys, chans, vol, cot, first, second, bottom, decode, final,
    vol_out, cot_out, w_first, w_second, w_bottom, w_decode, w_final,
    b_first, b_second, b_bottom, b_decode, b_final,
):
    c1, c2, c3 = chans
    y2, y3 = ys // 2, ys // 4
    for field, out in ((vol, vol_out), (cot, cot_out)):
        for x in range(xs):
            for y in range(ys):
                out[x, y * c1 : (y + 1) * c1, :] = field[:, x, y, :]
    for kernel, ahead, behind, count, ins, outs in (
        (first, w_first, b_first, ys, c1, c1),
        (second, w_second, b_second, y2, c1, c2),
        (bottom, w_bottom, b_bottom, y3, c2, c3),
        (decode, w_decode, b_decode, y2, c2, c1),
        (final, w_final, b_final, ys, c1, c1),
    ):
        ahead[...] = forward_matrix(kernel, count, ins, outs)
        for place, strip in enumerate(backward_strips(kernel, count, ins, outs)):
            behind[place * ins : (place + 1) * ins, :] = strip


def shards(
    wide_count, narrow_count,
    volume, cotangent, conv_first, conv_second, conv_bottom, lift_weight, conv_decode, conv_final
):
    c1, xs, ys, lanes = volume.shape
    c2, c3 = lift_weight.shape
    x2, y2, x3, y3 = xs // 2, ys // 2, xs // 4, ys // 4

    def back(field):
        return field.reshape(xs, ys, c1, lanes).transpose(2, 0, 1, 3)

    def edged(nx, ny, width):
        return pltpu.VMEM((nx + 2, (ny + 2) * width, lanes), BF)

    shape = jax.ShapeDtypeStruct((xs, ys * c1, lanes), BF)
    vmem = pl.BlockSpec(memory_space=pltpu.VMEM)
    call = pl.pallas_call(
        functools.partial(body, wide_count, narrow_count, xs, ys, (c1, c2, c3)),
        out_shape=(shape, shape),
        in_specs=[vmem] * 13,
        out_specs=(vmem, vmem),
        scratch_shapes=[
            edged(xs, ys, c1),
            edged(xs, ys, c1),
            edged(x2, y2, c1),
            edged(x3, y3, c2),
            edged(x2, y2, c2),
            edged(xs, ys, c1),
            edged(x2, y2, c1),
            edged(x3, y3, c3),
            edged(x2, y2, c2),
            edged(xs, ys, c1),
            pltpu.VMEM((xs, ys * c1, lanes), F32),
            pltpu.VMEM((xs, ys * c1, lanes), BF),
            pltpu.VMEM((xs, ys * c1, lanes), BF),
            pltpu.VMEM((x2, y2 * c2, lanes), F32),
            pltpu.VMEM((x2, y2 * c2, lanes), BF),
            pltpu.SemaphoreType.DMA((10, 8)),
            pltpu.SemaphoreType.DMA((10, 8)),
        ],
        compiler_params=pltpu.CompilerParams(
            collective_id=0, has_side_effects=True, vmem_limit_bytes=40 * 1024 * 1024
        ),
    )
    kernels = (conv_first, conv_second, conv_bottom, conv_decode, conv_final)
    counts = (ys, y2, y3, y2, ys)

    def matrix(count, ins, outs):
        return jax.ShapeDtypeStruct((3 * count * outs, 3 * (count + 2) * ins), BF)

    prepared = pl.pallas_call(
        functools.partial(prepare, xs, ys, (c1, c2, c3)),
        out_shape=(shape, shape)
        + tuple(matrix(n, k.shape[3], k.shape[4]) for n, k in zip(counts, kernels))
        + tuple(matrix(n, k.shape[4], k.shape[3]) for n, k in zip(counts, kernels)),
        in_specs=[vmem] * 7,
        out_specs=(vmem,) * 12,
        compiler_params=pltpu.CompilerParams(vmem_limit_bytes=40 * 1024 * 1024),
    )(volume, cotangent, *(k.reshape(27 * k.shape[3], k.shape[4]) for k in kernels))
    (vol, cot, w_first, w_second, w_bottom, w_decode, w_final) = prepared[:7]
    features, grad = call(
        vol, cot, w_first, w_second, w_bottom, lift_weight, w_decode, w_final,
        *prepared[7:],
    )
    return back(features), back(grad)


def solution(mesh):
    cells = P(None, "wide", "narrow", None)
    return jax.shard_map(
        functools.partial(shards, mesh.shape["wide"], mesh.shape["narrow"]),
        mesh=mesh,
        in_specs=(cells, cells, P(), P(), P(), P(), P(), P()),
        out_specs=(cells, cells),
        check_vma=False,
    )
```

```python
import functools

import jax
import jax.numpy as jnp
from jax import lax
from jax.experimental import pallas as pl
from jax.experimental.pallas import tpu as pltpu
from jax.sharding import PartitionSpec as P

BF = jnp.bfloat16
F32 = jnp.float32
SIDES = tuple((dx, dy) for dx in (-1, 0, 1) for dy in (-1, 0, 1) if (dx, dy) != (0, 0))


def sigmoid(value):
    return jax.nn.sigmoid(value)


def silu(value):
    return value * sigmoid(value)


def slope(value):
    sigma = sigmoid(value)
    return sigma * (1.0 + value * (1.0 - sigma))


def lane_of(value):
    return lax.broadcasted_iota(jnp.int32, value.shape, value.ndim - 1)


def conv(weights, edged, xs, step):
    lanes = edged.shape[2]
    depth = 3 * edged.shape[1]
    rows = weights.shape[0] // 3
    matrix = weights[...]
    outs = []
    for x in range(xs):
        part = jnp.dot(
            matrix, edged[x : x + 3].reshape(depth, lanes), preferred_element_type=F32
        )
        low, mid, high = part[:rows], part[rows : 2 * rows], part[2 * rows :]
        lane = lane_of(low)
        low = jnp.where(lane < step, 0.0, pltpu.roll(low, step, 1))
        high = jnp.where(lane >= lanes - step, 0.0, pltpu.roll(high, lanes - step, 1))
        outs.append(low + mid + high)
    return outs


def block_sum(fields, chans, step):
    outs = []
    for x in range(0, len(fields), 2):
        both = fields[x] + fields[x + 1]
        rows, lanes = both.shape
        both = jnp.concatenate(
            [
                both[y * chans : (y + 1) * chans] + both[(y + 1) * chans : (y + 2) * chans]
                for y in range(0, rows // chans, 2)
            ],
            axis=0,
        )
        lane = lane_of(both)
        other = jnp.where(
            lax.rem(lane // step, 2) == 0,
            pltpu.roll(both, lanes - step, 1),
            pltpu.roll(both, step, 1),
        )
        outs.append(both + other)
    return outs


def spread(fields, chans):
    outs = []
    for field in fields:
        parts = []
        for y in range(field.shape[0] // chans):
            cell = field[y * chans : (y + 1) * chans]
            parts += [cell, cell]
        wide = jnp.concatenate(parts, axis=0)
        outs += [wide, wide]
    return outs


def tap(kernel, ex, ey, ez, rows, flip):
    if flip:
        ex, ey, ez = 2 - ex, 2 - ey, 2 - ez
    return kernel[pl.ds(((ex * 3 + ey) * 3 + ez) * rows, rows), :]


def turned(out, kernel, ys, rows, columns, flip):
    zero = jnp.zeros((rows, columns), BF)
    strips = [
        jnp.concatenate(
            [
                tap(kernel, ex, rim - y, ez, rows, flip) if 0 <= rim - y < 3 else zero
                for ez in range(3)
                for y in range(ys)
            ],
            axis=1,
        )
        for ex in range(3)
        for rim in range(ys + 2)
    ]
    size = 3 * ys * columns
    row = lax.broadcasted_iota(jnp.int32, (size, size), 0)
    column = lax.broadcasted_iota(jnp.int32, (size, size), 1)
    eye = jnp.where(row == column, 1.0, 0.0).astype(BF)
    out[...] = lax.dot_general(
        eye,
        jnp.concatenate(strips, axis=0),
        (((1,), (1,)), ((), ())),
        preferred_element_type=F32,
    ).astype(BF)


def direct(out, kernel, ys, rows, columns, flip):
    zero = jnp.zeros((rows, columns), BF)
    for ez in range(3):
        for y in range(ys):
            place = (ez * ys + y) * rows
            out[place : place + rows, :] = jnp.concatenate(
                [
                    tap(kernel, ex, rim - y, ez, rows, flip) if 0 <= rim - y < 3 else zero
                    for ex in range(3)
                    for rim in range(ys + 2)
                ],
                axis=1,
            )


def body(
    wide_count, narrow_count, xs, ys, chans,
    vol_in, cot_in, first_in, second_in, bottom_in, lift_in, decode_in, final_in,
    features_ref, grad_ref,
    vol, cot, first, second, bottom, lift, decode, final,
    w_first, w_second, w_bottom, w_decode, w_final,
    b_first, b_second, b_bottom, b_decode, b_final,
    e_vol, e_cot, e_p1, e_p2, e_j2, e_j1, e_gd, e_gb, e_gs, e_gf,
    pre_first, hidden_first, grad_joined, pre_second, hidden_second,
    send_sem, recv_sem, load_sem,
):
    loads = [
        pltpu.make_async_copy(source, target, load_sem.at[place])
        for place, (source, target) in enumerate(
            (
                (vol_in, vol), (cot_in, cot), (first_in, first), (final_in, final),
                (second_in, second), (bottom_in, bottom), (lift_in, lift), (decode_in, decode),
            )
        )
    ]
    for load in loads:
        load.start()
    c1, c2, c3 = chans
    x2, y2 = xs // 2, ys // 2
    x3, y3 = x2 // 2, y2 // 2
    me_wide = lax.axis_index("wide")
    me_narrow = lax.axis_index("narrow")

    def exists(dx, dy):
        near_x, near_y = me_wide + dx, me_narrow + dy
        return (
            (near_x >= 0) & (near_x < wide_count) & (near_y >= 0) & (near_y < narrow_count)
        )

    def span(delta, count, sending):
        if delta == 0:
            return 1, count
        if sending:
            return (count if delta > 0 else 1), 1
        return (0 if delta > 0 else count + 1), 1

    def copy_of(index, edged, side, nx, ny, width):
        dx, dy = SIDES[side]

        def part(sending):
            x_at, x_len = span(dx, nx, sending)
            y_at, y_len = span(dy, ny, sending)
            return edged.at[pl.ds(x_at, x_len), pl.ds(y_at * width, y_len * width), :]

        return pltpu.make_async_remote_copy(
            src_ref=part(True),
            dst_ref=part(False),
            send_sem=send_sem.at[index, side],
            recv_sem=recv_sem.at[index, side],
            device_id=(me_wide + dx, me_narrow + dy),
            device_id_type=pl.DeviceIdType.MESH,
        )

    started = []

    def send(index, edged, nx, ny, width):
        for side, (dx, dy) in enumerate(SIDES):
            copy = copy_of(index, edged, side, nx, ny, width)
            pl.when(exists(dx, dy))(copy.start)
        started.append((index, edged, nx, ny, width))

    def receive(index, edged, nx, ny, width):
        for side, (dx, dy) in enumerate(SIDES):
            copy = copy_of(index, edged, side, nx, ny, width)
            pl.when(exists(-dx, -dy))(copy.wait_recv)

    def put(edged, fields, width):
        rows = fields[0].shape[0]
        for x, field in enumerate(fields):
            edged[x + 1, width : width + rows, :] = field.astype(BF)

    def clear(edged, nx, ny, width):
        lanes = edged.shape[2]
        edged[0] = jnp.zeros(((ny + 2) * width, lanes), BF)
        edged[nx + 1] = jnp.zeros(((ny + 2) * width, lanes), BF)
        for x in range(1, nx + 1):
            edged[x, 0:width, :] = jnp.zeros((width, lanes), BF)
            edged[x, (ny + 1) * width : (ny + 2) * width, :] = jnp.zeros((width, lanes), BF)

    spec_vol = (0, e_vol, xs, ys, c1)
    spec_cot = (1, e_cot, xs, ys, c1)
    spec_p1 = (2, e_p1, x2, y2, c1)
    spec_p2 = (3, e_p2, x3, y3, c2)
    spec_j2 = (4, e_j2, x2, y2, c2)
    spec_j1 = (5, e_j1, xs, ys, c1)
    spec_gd = (6, e_gd, x2, y2, c1)
    spec_gb = (7, e_gb, x3, y3, c3)
    spec_gs = (8, e_gs, x2, y2, c2)
    spec_gf = (9, e_gf, xs, ys, c1)
    for spec in (
        spec_vol, spec_cot, spec_p1, spec_p2, spec_j2, spec_j1, spec_gd, spec_gb, spec_gs, spec_gf
    ):
        clear(*spec[1:])

    barrier = pltpu.get_barrier_semaphore()
    for dx, dy in SIDES:

        @pl.when(exists(dx, dy))
        def _(dx=dx, dy=dy):
            pl.semaphore_signal(
                barrier,
                inc=1,
                device_id=(me_wide + dx, me_narrow + dy),
                device_id_type=pl.DeviceIdType.MESH,
            )

    for load, source, edged in ((loads[0], vol, e_vol), (loads[1], cot, e_cot)):
        load.wait()
        for x in range(xs):
            for y in range(ys):
                edged[x + 1, (y + 1) * c1 : (y + 2) * c1, :] = source[:, x, y, :]
    across = 1 + (me_wide > 0).astype(jnp.int32) + (me_wide < wide_count - 1).astype(jnp.int32)
    along = 1 + (me_narrow > 0).astype(jnp.int32) + (me_narrow < narrow_count - 1).astype(jnp.int32)
    pl.semaphore_wait(barrier, across * along - 1)

    send(*spec_vol)
    send(*spec_cot)

    loads[2].wait()
    turned(w_first, first, ys, c1, c1, False)
    receive(*spec_vol)
    hidden = []
    for x, pre in enumerate(conv(w_first, e_vol, xs, 1)):
        pre_first[x] = pre
        hidden.append(silu(pre).astype(BF))
        hidden_first[x] = hidden[-1]
    pooled = block_sum([h.astype(F32) for h in hidden], c1, 1)
    put(e_p1, [p * 0.125 for p in pooled], c1)
    send(*spec_p1)

    loads[3].wait()
    direct(b_final, final, ys, c1, c1, True)
    receive(*spec_cot)
    joined = [g.astype(BF) for g in conv(b_final, e_cot, xs, 1)]
    for x in range(xs):
        grad_joined[x] = joined[x]
    joined_sum = block_sum([g.astype(F32) for g in joined], c1, 1)

    loads[4].wait()
    turned(w_second, second, y2, c1, c2, False)
    receive(*spec_p1)
    hidden = []
    for x, pre in enumerate(conv(w_second, e_p1, x2, 2)):
        pre_second[x] = pre
        hidden.append(silu(pre).astype(BF))
        hidden_second[x] = hidden[-1]
    pooled = block_sum([h.astype(F32) for h in hidden], c2, 2)
    put(e_p2, [p * 0.125 for p in pooled], c2)
    send(*spec_p2)

    loads[5].wait()
    loads[6].wait()
    turned(w_bottom, bottom, y3, c2, c3, False)
    receive(*spec_p2)
    pre_bottom = conv(w_bottom, e_p2, x3, 4)
    lifted = []
    for pre in pre_bottom:
        hid = silu(pre).astype(BF)
        lifted.append(
            jnp.concatenate(
                [
                    jnp.dot(lift[...], hid[y * c3 : (y + 1) * c3], preferred_element_type=F32)
                    for y in range(y3)
                ],
                axis=0,
            )
        )
    lifted = spread(lifted, c2)
    put(e_j2, [lifted[x] + hidden_second[x].astype(F32) for x in range(x2)], c2)
    send(*spec_j2)

    loads[7].wait()
    direct(w_decode, decode, y2, c1, c2, False)
    receive(*spec_j2)
    pre_decode = conv(w_decode, e_j2, x2, 2)
    put(e_gd, [joined_sum[x] * slope(pre_decode[x]) for x in range(x2)], c1)
    send(*spec_gd)
    decoded = spread([silu(pre).astype(BF).astype(F32) for pre in pre_decode], c1)
    put(e_j1, [decoded[x] + hidden_first[x].astype(F32) for x in range(xs)], c1)
    send(*spec_j1)

    turned(b_decode, decode, y2, c1, c2, True)
    turned(w_final, final, ys, c1, c1, False)
    receive(*spec_gd)
    second_up = [g.astype(BF).astype(F32) for g in conv(b_decode, e_gd, x2, 2)]
    grad_lift = [g.astype(BF) for g in block_sum(second_up, c2, 2)]
    grad_bottom = []
    for x in range(x3):
        back = jnp.concatenate(
            [
                lax.dot_general(
                    lift[...],
                    grad_lift[x][y * c2 : (y + 1) * c2],
                    (((0,), (0,)), ((), ())),
                    preferred_element_type=F32,
                )
                for y in range(y3)
            ],
            axis=0,
        )
        grad_bottom.append(back * slope(pre_bottom[x]))
    put(e_gb, grad_bottom, c3)
    send(*spec_gb)

    receive(*spec_j1)
    for x, out in enumerate(conv(w_final, e_j1, xs, 1)):
        features_ref[x] = out.astype(BF)

    direct(b_bottom, bottom, y3, c2, c3, True)
    receive(*spec_gb)
    pool_second = spread(conv(b_bottom, e_gb, x3, 4), c2)
    put(
        e_gs,
        [(second_up[x] + pool_second[x] * 0.125) * slope(pre_second[x]) for x in range(x2)],
        c2,
    )
    send(*spec_gs)

    direct(b_second, second, y2, c1, c2, True)
    receive(*spec_gs)
    pool_first = spread(conv(b_second, e_gs, x2, 2), c1)
    put(
        e_gf,
        [
            (grad_joined[x].astype(F32) + pool_first[x] * 0.125) * slope(pre_first[x])
            for x in range(xs)
        ],
        c1,
    )
    send(*spec_gf)

    direct(b_first, first, ys, c1, c1, True)
    receive(*spec_gf)
    for x, out in enumerate(conv(b_first, e_gf, xs, 1)):
        grad_ref[x] = out.astype(BF)

    for index, edged, nx, ny, width in started:
        for side, (dx, dy) in enumerate(SIDES):
            copy = copy_of(index, edged, side, nx, ny, width)
            pl.when(exists(dx, dy))(copy.wait_send)


def shards(
    wide_count, narrow_count,
    volume, cotangent, conv_first, conv_second, conv_bottom, lift_weight, conv_decode, conv_final
):
    c1, xs, ys, lanes = volume.shape
    c2, c3 = lift_weight.shape
    x2, y2, x3, y3 = xs // 2, ys // 2, xs // 4, ys // 4

    def back(field):
        return field.reshape(xs, ys, c1, lanes).transpose(2, 0, 1, 3)

    def edged(nx, ny, width):
        return pltpu.VMEM((nx + 2, (ny + 2) * width, lanes), BF)

    def matrix(count, ins, outs):
        return pltpu.VMEM((3 * count * outs, 3 * (count + 2) * ins), BF)

    sizes = ((ys, c1, c1), (y2, c1, c2), (y3, c2, c3), (y2, c2, c1), (ys, c1, c1))
    first, second, bottom, decode, final = (
        k.reshape(27 * k.shape[3], k.shape[4])
        for k in (
            conv_first,
            conv_second,
            conv_bottom,
            conv_decode.transpose(0, 1, 2, 4, 3),
            conv_final,
        )
    )
    shape = jax.ShapeDtypeStruct((xs, ys * c1, lanes), BF)
    vmem = pl.BlockSpec(memory_space=pltpu.VMEM)
    call = pl.pallas_call(
        functools.partial(body, wide_count, narrow_count, xs, ys, (c1, c2, c3)),
        out_shape=(shape, shape),
        in_specs=[pl.BlockSpec(memory_space=pl.ANY)] * 8,
        out_specs=(vmem, vmem),
        scratch_shapes=[
            pltpu.VMEM(volume.shape, BF),
            pltpu.VMEM(cotangent.shape, BF),
            *(pltpu.VMEM(k.shape, BF) for k in (first, second, bottom, lift_weight, decode, final)),
            *(matrix(n, i, o) for n, i, o in sizes),
            *(matrix(n, o, i) for n, i, o in sizes),
            edged(xs, ys, c1),
            edged(xs, ys, c1),
            edged(x2, y2, c1),
            edged(x3, y3, c2),
            edged(x2, y2, c2),
            edged(xs, ys, c1),
            edged(x2, y2, c1),
            edged(x3, y3, c3),
            edged(x2, y2, c2),
            edged(xs, ys, c1),
            pltpu.VMEM((xs, ys * c1, lanes), F32),
            pltpu.VMEM((xs, ys * c1, lanes), BF),
            pltpu.VMEM((xs, ys * c1, lanes), BF),
            pltpu.VMEM((x2, y2 * c2, lanes), F32),
            pltpu.VMEM((x2, y2 * c2, lanes), BF),
            pltpu.SemaphoreType.DMA((10, 8)),
            pltpu.SemaphoreType.DMA((10, 8)),
            pltpu.SemaphoreType.DMA((8,)),
        ],
        compiler_params=pltpu.CompilerParams(
            collective_id=0, has_side_effects=True, vmem_limit_bytes=60 * 1024 * 1024
        ),
    )
    features, grad = call(
        volume, cotangent, first, second, bottom, lift_weight, decode, final
    )
    return back(features), back(grad)


def solution(mesh):
    cells = P(None, "wide", "narrow", None)
    return jax.shard_map(
        functools.partial(shards, mesh.shape["wide"], mesh.shape["narrow"]),
        mesh=mesh,
        in_specs=(cells, cells, P(), P(), P(), P(), P(), P()),
        out_specs=(cells, cells),
        check_vma=False,
    )
```

```python
import functools

import jax
import jax.numpy as jnp
from jax import lax
from jax.experimental import pallas as pl
from jax.experimental.pallas import tpu as pltpu
from jax.sharding import PartitionSpec as P

BF = jnp.bfloat16
F32 = jnp.float32
SIDES = tuple((dx, dy) for dx in (-1, 0, 1) for dy in (-1, 0, 1) if (dx, dy) != (0, 0))


def sigmoid(value):
    return jax.nn.sigmoid(value)


def silu(value):
    return value * sigmoid(value)


def slope(value):
    sigma = sigmoid(value)
    return sigma * (1.0 + value * (1.0 - sigma))


def lane_of(value):
    return lax.broadcasted_iota(jnp.int32, value.shape, value.ndim - 1)


def conv(weights, edged, xs, step):
    lanes = edged.shape[2]
    depth = 3 * edged.shape[1]
    rows = weights.shape[0] // 3
    matrix = weights[...]
    outs = []
    for x in range(xs):
        part = jnp.dot(
            matrix, edged[x : x + 3].reshape(depth, lanes), preferred_element_type=F32
        )
        low, mid, high = part[:rows], part[rows : 2 * rows], part[2 * rows :]
        lane = lane_of(low)
        low = jnp.where(lane < step, 0.0, pltpu.roll(low, step, 1))
        high = jnp.where(lane >= lanes - step, 0.0, pltpu.roll(high, lanes - step, 1))
        outs.append(low + mid + high)
    return outs


def block_sum(fields, chans, step):
    outs = []
    for x in range(0, len(fields), 2):
        both = fields[x] + fields[x + 1]
        rows, lanes = both.shape
        both = jnp.concatenate(
            [
                both[y * chans : (y + 1) * chans] + both[(y + 1) * chans : (y + 2) * chans]
                for y in range(0, rows // chans, 2)
            ],
            axis=0,
        )
        lane = lane_of(both)
        other = jnp.where(
            lax.rem(lane // step, 2) == 0,
            pltpu.roll(both, lanes - step, 1),
            pltpu.roll(both, step, 1),
        )
        outs.append(both + other)
    return outs


def spread(fields, chans):
    outs = []
    for field in fields:
        parts = []
        for y in range(field.shape[0] // chans):
            cell = field[y * chans : (y + 1) * chans]
            parts += [cell, cell]
        wide = jnp.concatenate(parts, axis=0)
        outs += [wide, wide]
    return outs


def tap(kernel, ex, ey, ez, rows, flip):
    if flip:
        ex, ey, ez = 2 - ex, 2 - ey, 2 - ez
    return kernel[pl.ds(((ex * 3 + ey) * 3 + ez) * rows, rows), :]


def turned(out, kernel, ys, rows, columns, flip):
    zero = jnp.zeros((rows, columns), BF)
    strips = [
        jnp.concatenate(
            [
                tap(kernel, ex, rim - y, ez, rows, flip) if 0 <= rim - y < 3 else zero
                for ez in range(3)
                for y in range(ys)
            ],
            axis=1,
        )
        for ex in range(3)
        for rim in range(ys + 2)
    ]
    size = 3 * ys * columns
    row = lax.broadcasted_iota(jnp.int32, (size, size), 0)
    column = lax.broadcasted_iota(jnp.int32, (size, size), 1)
    eye = jnp.where(row == column, 1.0, 0.0).astype(BF)
    out[...] = lax.dot_general(
        eye,
        jnp.concatenate(strips, axis=0),
        (((1,), (1,)), ((), ())),
        preferred_element_type=F32,
    ).astype(BF)


def direct(out, kernel, ys, rows, columns, flip):
    zero = jnp.zeros((rows, columns), BF)
    for ez in range(3):
        for y in range(ys):
            place = (ez * ys + y) * rows
            out[place : place + rows, :] = jnp.concatenate(
                [
                    tap(kernel, ex, rim - y, ez, rows, flip) if 0 <= rim - y < 3 else zero
                    for ex in range(3)
                    for rim in range(ys + 2)
                ],
                axis=1,
            )


def body(
    wide_count, narrow_count, xs, ys, chans,
    vol_in, cot_in, first_in, second_in, bottom_in, lift_in, decode_in, final_in,
    features_ref, grad_ref,
    vol, cot, first, second, bottom, lift, decode, final,
    w_first, w_second, w_bottom, w_decode, w_final,
    b_first, b_second, b_bottom, b_decode, b_final,
    e_vol, e_cot, e_p1, e_p2, e_j2, e_j1, e_gd, e_gb, e_gs, e_gf, e_js, e_gj, e_sl,
    hidden_first, pre_second, hidden_second,
    send_sem, recv_sem, load_sem,
):
    loads = [
        pltpu.make_async_copy(source, target, load_sem.at[place])
        for place, (source, target) in enumerate(
            (
                (vol_in, vol), (cot_in, cot), (first_in, first), (final_in, final),
                (second_in, second), (bottom_in, bottom), (lift_in, lift), (decode_in, decode),
            )
        )
    ]
    for load in loads:
        load.start()
    c1, c2, c3 = chans
    x2, y2 = xs // 2, ys // 2
    x3, y3 = x2 // 2, y2 // 2
    me_wide = lax.axis_index("wide")
    me_narrow = lax.axis_index("narrow")

    def exists(dx, dy):
        near_x, near_y = me_wide + dx, me_narrow + dy
        return (
            (near_x >= 0) & (near_x < wide_count) & (near_y >= 0) & (near_y < narrow_count)
        )

    def span(delta, count, halo, sending):
        if delta == 0:
            return halo, count
        if sending:
            return (count if delta > 0 else halo), halo
        return (0 if delta > 0 else count + halo), halo

    def copy_of(index, edged, side, nx, ny, width, halo):
        dx, dy = SIDES[side]

        def part(sending):
            x_at, x_len = span(dx, nx, halo, sending)
            y_at, y_len = span(dy, ny, halo, sending)
            return edged.at[pl.ds(x_at, x_len), pl.ds(y_at * width, y_len * width), :]

        return pltpu.make_async_remote_copy(
            src_ref=part(True),
            dst_ref=part(False),
            send_sem=send_sem.at[index, side],
            recv_sem=recv_sem.at[index, side],
            device_id=(me_wide + dx, me_narrow + dy),
            device_id_type=pl.DeviceIdType.MESH,
        )

    started = []

    def send(*spec):
        for side, (dx, dy) in enumerate(SIDES):
            copy = copy_of(*spec[:2], side, *spec[2:])
            pl.when(exists(dx, dy))(copy.start)
        started.append(spec)

    def receive(*spec):
        for side, (dx, dy) in enumerate(SIDES):
            copy = copy_of(*spec[:2], side, *spec[2:])
            pl.when(exists(-dx, -dy))(copy.wait_recv)

    def put(edged, fields, width, halo=1):
        rows = fields[0].shape[0]
        for x, field in enumerate(fields):
            edged[x + halo, halo * width : halo * width + rows, :] = field.astype(edged.dtype)

    def clear(edged, nx, ny, width, halo):
        lanes = edged.shape[2]
        whole = jnp.zeros(((ny + 2 * halo) * width, lanes), edged.dtype)
        rim = jnp.zeros((halo * width, lanes), edged.dtype)
        for x in range(halo):
            edged[x] = whole
            edged[nx + halo + x] = whole
        for x in range(halo, nx + halo):
            edged[x, 0 : halo * width, :] = rim
            edged[x, (ny + halo) * width : (ny + 2 * halo) * width, :] = rim

    spec_vol = (0, e_vol, xs, ys, c1, 1)
    spec_cot = (1, e_cot, xs, ys, c1, 1)
    spec_p1 = (2, e_p1, x2, y2, c1, 1)
    spec_p2 = (3, e_p2, x3, y3, c2, 1)
    spec_j2 = (4, e_j2, x2, y2, c2, 2)
    spec_j1 = (5, e_j1, xs, ys, c1, 1)
    spec_js = (6, e_js, x2, y2, c1, 1)
    spec_gb = (7, e_gb, x3, y3, c3, 1)
    spec_gs = (8, e_gs, x2, y2, c2, 2)
    spec_gj = (9, e_gj, xs, ys, c1, 1)
    spec_sl = (10, e_sl, xs, ys, c1, 1)
    for spec in (
        spec_vol, spec_cot, spec_p1, spec_p2, spec_j2, spec_j1, spec_js, spec_gb, spec_gs,
        spec_gj, spec_sl,
    ):
        clear(*spec[1:])

    barrier = pltpu.get_barrier_semaphore()
    for dx, dy in SIDES:

        @pl.when(exists(dx, dy))
        def _(dx=dx, dy=dy):
            pl.semaphore_signal(
                barrier,
                inc=1,
                device_id=(me_wide + dx, me_narrow + dy),
                device_id_type=pl.DeviceIdType.MESH,
            )

    for load, source, edged in ((loads[0], vol, e_vol), (loads[1], cot, e_cot)):
        load.wait()
        for x in range(xs):
            for y in range(ys):
                edged[x + 1, (y + 1) * c1 : (y + 2) * c1, :] = source[:, x, y, :]
    across = 1 + (me_wide > 0).astype(jnp.int32) + (me_wide < wide_count - 1).astype(jnp.int32)
    along = 1 + (me_narrow > 0).astype(jnp.int32) + (me_narrow < narrow_count - 1).astype(jnp.int32)
    pl.semaphore_wait(barrier, across * along - 1)

    send(*spec_vol)
    send(*spec_cot)

    loads[2].wait()
    turned(w_first, first, ys, c1, c1, False)
    receive(*spec_vol)
    hidden, slopes = [], []
    for x, pre in enumerate(conv(w_first, e_vol, xs, 1)):
        slopes.append(slope(pre))
        hidden.append(silu(pre).astype(BF))
        hidden_first[x] = hidden[-1]
    pooled = block_sum([h.astype(F32) for h in hidden], c1, 1)
    put(e_p1, [p * 0.125 for p in pooled], c1)
    send(*spec_p1)
    put(e_sl, slopes, c1)
    send(*spec_sl)

    loads[3].wait()
    direct(b_final, final, ys, c1, c1, True)
    receive(*spec_cot)
    joined = [g.astype(BF) for g in conv(b_final, e_cot, xs, 1)]
    put(e_gj, joined, c1)
    put(e_js, block_sum([g.astype(F32) for g in joined], c1, 1), c1)
    send(*spec_js)
    send(*spec_gj)

    loads[4].wait()
    turned(w_second, second, y2, c1, c2, False)
    receive(*spec_p1)
    hidden = []
    for x, pre in enumerate(conv(w_second, e_p1, x2, 2)):
        pre_second[x] = pre
        hidden.append(silu(pre).astype(BF))
        hidden_second[x] = hidden[-1]
    pooled = block_sum([h.astype(F32) for h in hidden], c2, 2)
    put(e_p2, [p * 0.125 for p in pooled], c2)
    send(*spec_p2)

    loads[5].wait()
    loads[6].wait()
    turned(w_bottom, bottom, y3, c2, c3, False)
    receive(*spec_p2)
    pre_bottom = conv(w_bottom, e_p2, x3, 4)
    lifted = []
    for pre in pre_bottom:
        hid = silu(pre).astype(BF)
        lifted.append(
            jnp.concatenate(
                [
                    jnp.dot(lift[...], hid[y * c3 : (y + 1) * c3], preferred_element_type=F32)
                    for y in range(y3)
                ],
                axis=0,
            )
        )
    lifted = spread(lifted, c2)
    put(e_j2, [lifted[x] + hidden_second[x].astype(F32) for x in range(x2)], c2, 2)
    send(*spec_j2)

    loads[7].wait()
    direct(w_decode, decode, y2 + 2, c1, c2, False)
    turned(b_decode, decode, y2, c1, c2, True)
    receive(*spec_j2)
    pre_decode = conv(w_decode, e_j2, x2 + 2, 2)
    inner = [pre[c1 : (y2 + 1) * c1] for pre in pre_decode[1:-1]]
    decoded = spread([silu(pre).astype(BF).astype(F32) for pre in inner], c1)
    put(e_j1, [decoded[x] + hidden_first[x].astype(F32) for x in range(xs)], c1)
    send(*spec_j1)

    receive(*spec_js)
    for x in range(x2 + 2):
        e_gd[x] = (e_js[x] * slope(pre_decode[x])).astype(BF)
    second_up = [g.astype(BF).astype(F32) for g in conv(b_decode, e_gd, x2, 2)]
    grad_lift = [g.astype(BF) for g in block_sum(second_up, c2, 2)]
    grad_bottom = []
    for x in range(x3):
        back = jnp.concatenate(
            [
                lax.dot_general(
                    lift[...],
                    grad_lift[x][y * c2 : (y + 1) * c2],
                    (((0,), (0,)), ((), ())),
                    preferred_element_type=F32,
                )
                for y in range(y3)
            ],
            axis=0,
        )
        grad_bottom.append(back * slope(pre_bottom[x]))
    put(e_gb, grad_bottom, c3)
    send(*spec_gb)

    turned(w_final, final, ys, c1, c1, False)
    receive(*spec_j1)
    for x, out in enumerate(conv(w_final, e_j1, xs, 1)):
        features_ref[x] = out.astype(BF)

    direct(b_bottom, bottom, y3, c2, c3, True)
    receive(*spec_gb)
    pool_second = spread(conv(b_bottom, e_gb, x3, 4), c2)
    put(
        e_gs,
        [(second_up[x] + pool_second[x] * 0.125) * slope(pre_second[x]) for x in range(x2)],
        c2,
        2,
    )
    send(*spec_gs)

    direct(b_second, second, y2 + 2, c1, c2, True)
    direct(b_first, first, ys, c1, c1, True)
    receive(*spec_gs)
    pool_first = spread(conv(b_second, e_gs, x2 + 2, 2), c1)
    receive(*spec_gj)
    receive(*spec_sl)
    for x in range(xs + 2):
        lower = pool_first[x + 1][c1 : (ys + 3) * c1]
        e_gf[x] = ((e_gj[x].astype(F32) + lower * 0.125) * e_sl[x]).astype(BF)
    for x, out in enumerate(conv(b_first, e_gf, xs, 1)):
        grad_ref[x] = out.astype(BF)

    for spec in started:
        for side, (dx, dy) in enumerate(SIDES):
            copy = copy_of(*spec[:2], side, *spec[2:])
            pl.when(exists(dx, dy))(copy.wait_send)


def shards(
    wide_count, narrow_count,
    volume, cotangent, conv_first, conv_second, conv_bottom, lift_weight, conv_decode, conv_final
):
    c1, xs, ys, lanes = volume.shape
    c2, c3 = lift_weight.shape
    x2, y2, x3, y3 = xs // 2, ys // 2, xs // 4, ys // 4

    def back(field):
        return field.reshape(xs, ys, c1, lanes).transpose(2, 0, 1, 3)

    def edged(nx, ny, width, halo=1, kind=BF):
        return pltpu.VMEM((nx + 2 * halo, (ny + 2 * halo) * width, lanes), kind)

    def matrix(count, ins, outs):
        return pltpu.VMEM((3 * count * outs, 3 * (count + 2) * ins), BF)

    first, second, bottom, decode, final = (
        k.reshape(27 * k.shape[3], k.shape[4])
        for k in (
            conv_first,
            conv_second,
            conv_bottom,
            conv_decode.transpose(0, 1, 2, 4, 3),
            conv_final,
        )
    )
    shape = jax.ShapeDtypeStruct((xs, ys * c1, lanes), BF)
    vmem = pl.BlockSpec(memory_space=pltpu.VMEM)
    call = pl.pallas_call(
        functools.partial(body, wide_count, narrow_count, xs, ys, (c1, c2, c3)),
        out_shape=(shape, shape),
        in_specs=[pl.BlockSpec(memory_space=pl.ANY)] * 8,
        out_specs=(vmem, vmem),
        scratch_shapes=[
            pltpu.VMEM(volume.shape, BF),
            pltpu.VMEM(cotangent.shape, BF),
            *(pltpu.VMEM(k.shape, BF) for k in (first, second, bottom, lift_weight, decode, final)),
            matrix(ys, c1, c1),
            matrix(y2, c1, c2),
            matrix(y3, c2, c3),
            matrix(y2 + 2, c2, c1),
            matrix(ys, c1, c1),
            matrix(ys, c1, c1),
            matrix(y2 + 2, c2, c1),
            matrix(y3, c3, c2),
            matrix(y2, c1, c2),
            matrix(ys, c1, c1),
            edged(xs, ys, c1),
            edged(xs, ys, c1),
            edged(x2, y2, c1),
            edged(x3, y3, c2),
            edged(x2, y2, c2, 2),
            edged(xs, ys, c1),
            edged(x2, y2, c1),
            edged(x3, y3, c3),
            edged(x2, y2, c2, 2),
            edged(xs, ys, c1),
            edged(x2, y2, c1, 1, F32),
            edged(xs, ys, c1),
            edged(xs, ys, c1, 1, F32),
            pltpu.VMEM((xs, ys * c1, lanes), BF),
            pltpu.VMEM((x2, y2 * c2, lanes), F32),
            pltpu.VMEM((x2, y2 * c2, lanes), BF),
            pltpu.SemaphoreType.DMA((11, 8)),
            pltpu.SemaphoreType.DMA((11, 8)),
            pltpu.SemaphoreType.DMA((8,)),
        ],
        compiler_params=pltpu.CompilerParams(
            collective_id=0, has_side_effects=True, vmem_limit_bytes=60 * 1024 * 1024
        ),
    )
    features, grad = call(
        volume, cotangent, first, second, bottom, lift_weight, decode, final
    )
    return back(features), back(grad)


def solution(mesh):
    cells = P(None, "wide", "narrow", None)
    return jax.shard_map(
        functools.partial(shards, mesh.shape["wide"], mesh.shape["narrow"]),
        mesh=mesh,
        in_specs=(cells, cells, P(), P(), P(), P(), P(), P()),
        out_specs=(cells, cells),
        check_vma=False,
    )
```

```python
import functools

import jax
import jax.numpy as jnp
from jax import lax
from jax.experimental import pallas as pl
from jax.experimental.pallas import tpu as pltpu
from jax.sharding import PartitionSpec as P

BF = jnp.bfloat16
F32 = jnp.float32
SIDES = tuple((dx, dy) for dx in (-1, 0, 1) for dy in (-1, 0, 1) if (dx, dy) != (0, 0))


def sigmoid(value):
    return jax.nn.sigmoid(value)


def silu(value):
    return value * sigmoid(value)


def slope(value):
    sigma = sigmoid(value)
    return sigma * (1.0 + value * (1.0 - sigma))


def lane_of(value):
    return lax.broadcasted_iota(jnp.int32, value.shape, value.ndim - 1)


def conv(weights, edged, xs, step):
    lanes = edged.shape[2]
    depth = 3 * edged.shape[1]
    rows = weights.shape[0] // 3
    matrix = weights[...]
    outs = []
    parts = []
    for first in range(0, xs, 2):
        group = range(first, min(first + 2, xs))
        wide = jnp.concatenate([edged[x : x + 3].reshape(depth, lanes) for x in group], axis=1)
        both = jnp.dot(matrix, wide, preferred_element_type=F32)
        parts += [both[:, place * lanes : (place + 1) * lanes] for place in range(len(group))]
    for part in parts:
        low, mid, high = part[:rows], part[rows : 2 * rows], part[2 * rows :]
        lane = lane_of(low)
        low = jnp.where(lane < step, 0.0, pltpu.roll(low, step, 1))
        high = jnp.where(lane >= lanes - step, 0.0, pltpu.roll(high, lanes - step, 1))
        outs.append(low + mid + high)
    return outs


def block_sum(fields, chans, step):
    outs = []
    for x in range(0, len(fields), 2):
        both = fields[x] + fields[x + 1]
        rows, lanes = both.shape
        both = jnp.concatenate(
            [
                both[y * chans : (y + 1) * chans] + both[(y + 1) * chans : (y + 2) * chans]
                for y in range(0, rows // chans, 2)
            ],
            axis=0,
        )
        lane = lane_of(both)
        other = jnp.where(
            lax.rem(lane // step, 2) == 0,
            pltpu.roll(both, lanes - step, 1),
            pltpu.roll(both, step, 1),
        )
        outs.append(both + other)
    return outs


def spread(fields, chans):
    outs = []
    for field in fields:
        parts = []
        for y in range(field.shape[0] // chans):
            cell = field[y * chans : (y + 1) * chans]
            parts += [cell, cell]
        wide = jnp.concatenate(parts, axis=0)
        outs += [wide, wide]
    return outs


def tap(kernel, ex, ey, ez, rows, flip):
    if flip:
        ex, ey, ez = 2 - ex, 2 - ey, 2 - ez
    return kernel[pl.ds(((ex * 3 + ey) * 3 + ez) * rows, rows), :]


def turned(out, kernel, ys, rows, columns, flip):
    zero = jnp.zeros((rows, columns), BF)
    strips = [
        jnp.concatenate(
            [
                tap(kernel, ex, rim - y, ez, rows, flip) if 0 <= rim - y < 3 else zero
                for ez in range(3)
                for y in range(ys)
            ],
            axis=1,
        )
        for ex in range(3)
        for rim in range(ys + 2)
    ]
    size = 3 * ys * columns
    row = lax.broadcasted_iota(jnp.int32, (size, size), 0)
    column = lax.broadcasted_iota(jnp.int32, (size, size), 1)
    eye = jnp.where(row == column, 1.0, 0.0).astype(BF)
    out[...] = lax.dot_general(
        eye,
        jnp.concatenate(strips, axis=0),
        (((1,), (1,)), ((), ())),
        preferred_element_type=F32,
    ).astype(BF)


def direct(out, kernel, ys, rows, columns, flip):
    zero = jnp.zeros((rows, columns), BF)
    for ez in range(3):
        for y in range(ys):
            place = (ez * ys + y) * rows
            out[place : place + rows, :] = jnp.concatenate(
                [
                    tap(kernel, ex, rim - y, ez, rows, flip) if 0 <= rim - y < 3 else zero
                    for ex in range(3)
                    for rim in range(ys + 2)
                ],
                axis=1,
            )


def body(
    wide_count, narrow_count, xs, ys, chans,
    vol_in, cot_in, first_in, second_in, bottom_in, lift_in, decode_in, final_in,
    features_ref, grad_ref,
    vol, cot, first, second, bottom, lift, decode, final,
    w_first, w_second, w_bottom, w_decode, w_final,
    b_first, b_second, b_bottom, b_decode, b_final,
    e_vol, e_cot, e_p1, e_p2, e_j2, e_j1, e_gd, e_gb, e_gs, e_gf, e_js, e_gj, e_sl,
    hidden_first, pre_second, hidden_second,
    send_sem, recv_sem, load_sem,
):
    loads = [
        pltpu.make_async_copy(source, target, load_sem.at[place])
        for place, (source, target) in enumerate(
            (
                (vol_in, vol), (cot_in, cot), (first_in, first), (final_in, final),
                (second_in, second), (bottom_in, bottom), (lift_in, lift), (decode_in, decode),
            )
        )
    ]
    for load in loads:
        load.start()
    c1, c2, c3 = chans
    x2, y2 = xs // 2, ys // 2
    x3, y3 = x2 // 2, y2 // 2
    me_wide = lax.axis_index("wide")
    me_narrow = lax.axis_index("narrow")

    def exists(dx, dy):
        near_x, near_y = me_wide + dx, me_narrow + dy
        return (
            (near_x >= 0) & (near_x < wide_count) & (near_y >= 0) & (near_y < narrow_count)
        )

    def span(delta, count, halo, sending):
        if delta == 0:
            return halo, count
        if sending:
            return (count if delta > 0 else halo), halo
        return (0 if delta > 0 else count + halo), halo

    def copy_of(index, edged, side, nx, ny, width, halo):
        dx, dy = SIDES[side]

        def part(sending):
            x_at, x_len = span(dx, nx, halo, sending)
            y_at, y_len = span(dy, ny, halo, sending)
            return edged.at[pl.ds(x_at, x_len), pl.ds(y_at * width, y_len * width), :]

        return pltpu.make_async_remote_copy(
            src_ref=part(True),
            dst_ref=part(False),
            send_sem=send_sem.at[index, side],
            recv_sem=recv_sem.at[index, side],
            device_id=(me_wide + dx, me_narrow + dy),
            device_id_type=pl.DeviceIdType.MESH,
        )

    started = []

    def send(*spec):
        for side, (dx, dy) in enumerate(SIDES):
            copy = copy_of(*spec[:2], side, *spec[2:])
            pl.when(exists(dx, dy))(copy.start)
        started.append(spec)

    def receive(*spec):
        for side, (dx, dy) in enumerate(SIDES):
            copy = copy_of(*spec[:2], side, *spec[2:])
            pl.when(exists(-dx, -dy))(copy.wait_recv)

    def put(edged, fields, width, halo=1):
        rows = fields[0].shape[0]
        for x, field in enumerate(fields):
            edged[x + halo, halo * width : halo * width + rows, :] = field.astype(edged.dtype)

    def clear(edged, nx, ny, width, halo):
        lanes = edged.shape[2]
        whole = jnp.zeros(((ny + 2 * halo) * width, lanes), edged.dtype)
        rim = jnp.zeros((halo * width, lanes), edged.dtype)
        for x in range(halo):
            edged[x] = whole
            edged[nx + halo + x] = whole
        for x in range(halo, nx + halo):
            edged[x, 0 : halo * width, :] = rim
            edged[x, (ny + halo) * width : (ny + 2 * halo) * width, :] = rim

    spec_vol = (0, e_vol, xs, ys, c1, 1)
    spec_cot = (1, e_cot, xs, ys, c1, 1)
    spec_p1 = (2, e_p1, x2, y2, c1, 1)
    spec_p2 = (3, e_p2, x3, y3, c2, 1)
    spec_j2 = (4, e_j2, x2, y2, c2, 2)
    spec_j1 = (5, e_j1, xs, ys, c1, 1)
    spec_js = (6, e_js, x2, y2, c1, 1)
    spec_gb = (7, e_gb, x3, y3, c3, 1)
    spec_gs = (8, e_gs, x2, y2, c2, 2)
    spec_gj = (9, e_gj, xs, ys, c1, 1)
    spec_sl = (10, e_sl, xs, ys, c1, 1)
    for spec in (
        spec_vol, spec_cot, spec_p1, spec_p2, spec_j2, spec_j1, spec_js, spec_gb, spec_gs,
        spec_gj, spec_sl,
    ):
        clear(*spec[1:])

    barrier = pltpu.get_barrier_semaphore()
    for dx, dy in SIDES:

        @pl.when(exists(dx, dy))
        def _(dx=dx, dy=dy):
            pl.semaphore_signal(
                barrier,
                inc=1,
                device_id=(me_wide + dx, me_narrow + dy),
                device_id_type=pl.DeviceIdType.MESH,
            )

    for load, source, edged in ((loads[0], vol, e_vol), (loads[1], cot, e_cot)):
        load.wait()
        for x in range(xs):
            for y in range(ys):
                edged[x + 1, (y + 1) * c1 : (y + 2) * c1, :] = source[:, x, y, :]
    across = 1 + (me_wide > 0).astype(jnp.int32) + (me_wide < wide_count - 1).astype(jnp.int32)
    along = 1 + (me_narrow > 0).astype(jnp.int32) + (me_narrow < narrow_count - 1).astype(jnp.int32)
    pl.semaphore_wait(barrier, across * along - 1)

    send(*spec_vol)
    send(*spec_cot)

    loads[2].wait()
    turned(w_first, first, ys, c1, c1, False)
    receive(*spec_vol)
    hidden, slopes = [], []
    for x, pre in enumerate(conv(w_first, e_vol, xs, 1)):
        slopes.append(slope(pre))
        hidden.append(silu(pre).astype(BF))
        hidden_first[x] = hidden[-1]
    pooled = block_sum([h.astype(F32) for h in hidden], c1, 1)
    put(e_p1, [p * 0.125 for p in pooled], c1)
    send(*spec_p1)
    put(e_sl, slopes, c1)
    send(*spec_sl)

    loads[3].wait()
    direct(b_final, final, ys, c1, c1, True)
    receive(*spec_cot)
    joined = [g.astype(BF) for g in conv(b_final, e_cot, xs, 1)]
    put(e_gj, joined, c1)
    put(e_js, block_sum([g.astype(F32) for g in joined], c1, 1), c1)
    send(*spec_js)
    send(*spec_gj)

    loads[4].wait()
    turned(w_second, second, y2, c1, c2, False)
    receive(*spec_p1)
    hidden = []
    for x, pre in enumerate(conv(w_second, e_p1, x2, 2)):
        pre_second[x] = pre
        hidden.append(silu(pre).astype(BF))
        hidden_second[x] = hidden[-1]
    pooled = block_sum([h.astype(F32) for h in hidden], c2, 2)
    put(e_p2, [p * 0.125 for p in pooled], c2)
    send(*spec_p2)

    loads[5].wait()
    loads[6].wait()
    turned(w_bottom, bottom, y3, c2, c3, False)
    receive(*spec_p2)
    pre_bottom = conv(w_bottom, e_p2, x3, 4)
    lifted = []
    for pre in pre_bottom:
        hid = silu(pre).astype(BF)
        lifted.append(
            jnp.concatenate(
                [
                    jnp.dot(lift[...], hid[y * c3 : (y + 1) * c3], preferred_element_type=F32)
                    for y in range(y3)
                ],
                axis=0,
            )
        )
    lifted = spread(lifted, c2)
    put(e_j2, [lifted[x] + hidden_second[x].astype(F32) for x in range(x2)], c2, 2)
    send(*spec_j2)

    loads[7].wait()
    direct(w_decode, decode, y2 + 2, c1, c2, False)
    turned(b_decode, decode, y2, c1, c2, True)
    receive(*spec_j2)
    pre_decode = conv(w_decode, e_j2, x2 + 2, 2)
    inner = [pre[c1 : (y2 + 1) * c1] for pre in pre_decode[1:-1]]
    decoded = spread([silu(pre).astype(BF).astype(F32) for pre in inner], c1)
    put(e_j1, [decoded[x] + hidden_first[x].astype(F32) for x in range(xs)], c1)
    send(*spec_j1)

    receive(*spec_js)
    for x in range(x2 + 2):
        e_gd[x] = (e_js[x] * slope(pre_decode[x])).astype(BF)
    second_up = [g.astype(BF).astype(F32) for g in conv(b_decode, e_gd, x2, 2)]
    grad_lift = [g.astype(BF) for g in block_sum(second_up, c2, 2)]
    grad_bottom = []
    for x in range(x3):
        back = jnp.concatenate(
            [
                lax.dot_general(
                    lift[...],
                    grad_lift[x][y * c2 : (y + 1) * c2],
                    (((0,), (0,)), ((), ())),
                    preferred_element_type=F32,
                )
                for y in range(y3)
            ],
            axis=0,
        )
        grad_bottom.append(back * slope(pre_bottom[x]))
    put(e_gb, grad_bottom, c3)
    send(*spec_gb)

    turned(w_final, final, ys, c1, c1, False)
    receive(*spec_j1)
    for x, out in enumerate(conv(w_final, e_j1, xs, 1)):
        features_ref[x] = out.astype(BF)

    direct(b_bottom, bottom, y3, c2, c3, True)
    receive(*spec_gb)
    pool_second = spread(conv(b_bottom, e_gb, x3, 4), c2)
    put(
        e_gs,
        [(second_up[x] + pool_second[x] * 0.125) * slope(pre_second[x]) for x in range(x2)],
        c2,
        2,
    )
    send(*spec_gs)

    direct(b_second, second, y2 + 2, c1, c2, True)
    direct(b_first, first, ys, c1, c1, True)
    receive(*spec_gs)
    pool_first = spread(conv(b_second, e_gs, x2 + 2, 2), c1)
    receive(*spec_gj)
    receive(*spec_sl)
    for x in range(xs + 2):
        lower = pool_first[x + 1][c1 : (ys + 3) * c1]
        e_gf[x] = ((e_gj[x].astype(F32) + lower * 0.125) * e_sl[x]).astype(BF)
    for x, out in enumerate(conv(b_first, e_gf, xs, 1)):
        grad_ref[x] = out.astype(BF)

    for spec in started:
        for side, (dx, dy) in enumerate(SIDES):
            copy = copy_of(*spec[:2], side, *spec[2:])
            pl.when(exists(dx, dy))(copy.wait_send)


def shards(
    wide_count, narrow_count,
    volume, cotangent, conv_first, conv_second, conv_bottom, lift_weight, conv_decode, conv_final
):
    c1, xs, ys, lanes = volume.shape
    c2, c3 = lift_weight.shape
    x2, y2, x3, y3 = xs // 2, ys // 2, xs // 4, ys // 4

    def back(field):
        return field.reshape(xs, ys, c1, lanes).transpose(2, 0, 1, 3)

    def edged(nx, ny, width, halo=1, kind=BF):
        return pltpu.VMEM((nx + 2 * halo, (ny + 2 * halo) * width, lanes), kind)

    def matrix(count, ins, outs):
        return pltpu.VMEM((3 * count * outs, 3 * (count + 2) * ins), BF)

    first, second, bottom, decode, final = (
        k.reshape(27 * k.shape[3], k.shape[4])
        for k in (
            conv_first,
            conv_second,
            conv_bottom,
            conv_decode.transpose(0, 1, 2, 4, 3),
            conv_final,
        )
    )
    shape = jax.ShapeDtypeStruct((xs, ys * c1, lanes), BF)
    vmem = pl.BlockSpec(memory_space=pltpu.VMEM)
    call = pl.pallas_call(
        functools.partial(body, wide_count, narrow_count, xs, ys, (c1, c2, c3)),
        out_shape=(shape, shape),
        in_specs=[pl.BlockSpec(memory_space=pl.ANY)] * 8,
        out_specs=(vmem, vmem),
        scratch_shapes=[
            pltpu.VMEM(volume.shape, BF),
            pltpu.VMEM(cotangent.shape, BF),
            *(pltpu.VMEM(k.shape, BF) for k in (first, second, bottom, lift_weight, decode, final)),
            matrix(ys, c1, c1),
            matrix(y2, c1, c2),
            matrix(y3, c2, c3),
            matrix(y2 + 2, c2, c1),
            matrix(ys, c1, c1),
            matrix(ys, c1, c1),
            matrix(y2 + 2, c2, c1),
            matrix(y3, c3, c2),
            matrix(y2, c1, c2),
            matrix(ys, c1, c1),
            edged(xs, ys, c1),
            edged(xs, ys, c1),
            edged(x2, y2, c1),
            edged(x3, y3, c2),
            edged(x2, y2, c2, 2),
            edged(xs, ys, c1),
            edged(x2, y2, c1),
            edged(x3, y3, c3),
            edged(x2, y2, c2, 2),
            edged(xs, ys, c1),
            edged(x2, y2, c1, 1, F32),
            edged(xs, ys, c1),
            edged(xs, ys, c1, 1, F32),
            pltpu.VMEM((xs, ys * c1, lanes), BF),
            pltpu.VMEM((x2, y2 * c2, lanes), F32),
            pltpu.VMEM((x2, y2 * c2, lanes), BF),
            pltpu.SemaphoreType.DMA((11, 8)),
            pltpu.SemaphoreType.DMA((11, 8)),
            pltpu.SemaphoreType.DMA((8,)),
        ],
        compiler_params=pltpu.CompilerParams(
            collective_id=0, has_side_effects=True, vmem_limit_bytes=60 * 1024 * 1024
        ),
    )
    features, grad = call(
        volume, cotangent, first, second, bottom, lift_weight, decode, final
    )
    return back(features), back(grad)


def solution(mesh):
    cells = P(None, "wide", "narrow", None)
    return jax.shard_map(
        functools.partial(shards, mesh.shape["wide"], mesh.shape["narrow"]),
        mesh=mesh,
        in_specs=(cells, cells, P(), P(), P(), P(), P(), P()),
        out_specs=(cells, cells),
        check_vma=False,
    )
```

```python
import functools

import jax
import jax.numpy as jnp
from jax import lax
from jax.experimental import pallas as pl
from jax.experimental.pallas import tpu as pltpu
from jax.sharding import PartitionSpec as P

BF = jnp.bfloat16
F32 = jnp.float32
SIDES = tuple((dx, dy) for dx in (-1, 0, 1) for dy in (-1, 0, 1) if (dx, dy) != (0, 0))


def sigmoid(value):
    return jax.nn.sigmoid(value)


def silu(value):
    return value * sigmoid(value)


def slope(value):
    sigma = sigmoid(value)
    return sigma * (1.0 + value * (1.0 - sigma))


def lane_of(value):
    return lax.broadcasted_iota(jnp.int32, value.shape, value.ndim - 1)


def conv(weights, edged, xs, step):
    lanes = edged.shape[2]
    depth = 3 * edged.shape[1]
    rows = weights.shape[0] // 3
    matrix = weights[...]
    outs = []
    parts = []
    for first in range(0, xs, 2):
        group = range(first, min(first + 2, xs))
        wide = jnp.concatenate([edged[x : x + 3].reshape(depth, lanes) for x in group], axis=1)
        both = jnp.dot(matrix, wide, preferred_element_type=F32)
        parts += [both[:, place * lanes : (place + 1) * lanes] for place in range(len(group))]
    for part in parts:
        low, mid, high = part[:rows], part[rows : 2 * rows], part[2 * rows :]
        lane = lane_of(low)
        low = jnp.where(lane < step, 0.0, pltpu.roll(low, step, 1))
        high = jnp.where(lane >= lanes - step, 0.0, pltpu.roll(high, lanes - step, 1))
        outs.append(low + mid + high)
    return outs


def block_sum(fields, chans, step):
    outs = []
    for x in range(0, len(fields), 2):
        both = fields[x] + fields[x + 1]
        rows, lanes = both.shape
        both = jnp.concatenate(
            [
                both[y * chans : (y + 1) * chans] + both[(y + 1) * chans : (y + 2) * chans]
                for y in range(0, rows // chans, 2)
            ],
            axis=0,
        )
        lane = lane_of(both)
        other = jnp.where(
            lax.rem(lane // step, 2) == 0,
            pltpu.roll(both, lanes - step, 1),
            pltpu.roll(both, step, 1),
        )
        outs.append(both + other)
    return outs


def spread(fields, chans):
    outs = []
    for field in fields:
        parts = []
        for y in range(field.shape[0] // chans):
            cell = field[y * chans : (y + 1) * chans]
            parts += [cell, cell]
        wide = jnp.concatenate(parts, axis=0)
        outs += [wide, wide]
    return outs


def tap(kernel, ex, ey, ez, rows, flip):
    if flip:
        ex, ey, ez = 2 - ex, 2 - ey, 2 - ez
    return kernel[pl.ds(((ex * 3 + ey) * 3 + ez) * rows, rows), :]


def turned(out, kernel, ys, rows, columns, flip):
    zero = jnp.zeros((rows, columns), BF)
    strips = [
        jnp.concatenate(
            [
                tap(kernel, ex, rim - y, ez, rows, flip) if 0 <= rim - y < 3 else zero
                for ez in range(3)
                for y in range(ys)
            ],
            axis=1,
        )
        for ex in range(3)
        for rim in range(ys + 2)
    ]
    size = 3 * ys * columns
    row = lax.broadcasted_iota(jnp.int32, (size, size), 0)
    column = lax.broadcasted_iota(jnp.int32, (size, size), 1)
    eye = jnp.where(row == column, 1.0, 0.0).astype(BF)
    out[...] = lax.dot_general(
        eye,
        jnp.concatenate(strips, axis=0),
        (((1,), (1,)), ((), ())),
        preferred_element_type=F32,
    ).astype(BF)


def direct(out, kernel, ys, rows, columns, flip):
    zero = jnp.zeros((rows, columns), BF)
    for ez in range(3):
        for y in range(ys):
            place = (ez * ys + y) * rows
            out[place : place + rows, :] = jnp.concatenate(
                [
                    tap(kernel, ex, rim - y, ez, rows, flip) if 0 <= rim - y < 3 else zero
                    for ex in range(3)
                    for rim in range(ys + 2)
                ],
                axis=1,
            )


def body(
    wide_count, narrow_count, xs, ys, chans,
    vol_in, cot_in, first_in, second_in, bottom_in, lift_in, decode_in, final_in,
    features_ref, grad_ref,
    vol, cot, first, second, bottom, lift, decode, final,
    w_first, w_second, w_bottom, w_decode, w_final,
    b_first, b_second, b_bottom, b_decode, b_final,
    e_vol, e_cot, e_p1, e_p2, e_j2, e_j1, e_gd, e_gb, e_gs, e_gf,
    pre_first, hidden_first, grad_joined, pre_second, hidden_second,
    send_sem, recv_sem, load_sem,
):
    loads = [
        pltpu.make_async_copy(source, target, load_sem.at[place])
        for place, (source, target) in enumerate(
            (
                (vol_in, vol), (cot_in, cot), (first_in, first), (final_in, final),
                (second_in, second), (bottom_in, bottom), (lift_in, lift), (decode_in, decode),
            )
        )
    ]
    for load in loads:
        load.start()
    c1, c2, c3 = chans
    x2, y2 = xs // 2, ys // 2
    x3, y3 = x2 // 2, y2 // 2
    me_wide = lax.axis_index("wide")
    me_narrow = lax.axis_index("narrow")

    def exists(dx, dy):
        near_x, near_y = me_wide + dx, me_narrow + dy
        return (
            (near_x >= 0) & (near_x < wide_count) & (near_y >= 0) & (near_y < narrow_count)
        )

    def span(delta, count, sending):
        if delta == 0:
            return 1, count
        if sending:
            return (count if delta > 0 else 1), 1
        return (0 if delta > 0 else count + 1), 1

    def copy_of(index, edged, side, nx, ny, width):
        dx, dy = SIDES[side]

        def part(sending):
            x_at, x_len = span(dx, nx, sending)
            y_at, y_len = span(dy, ny, sending)
            return edged.at[pl.ds(x_at, x_len), pl.ds(y_at * width, y_len * width), :]

        return pltpu.make_async_remote_copy(
            src_ref=part(True),
            dst_ref=part(False),
            send_sem=send_sem.at[index, side],
            recv_sem=recv_sem.at[index, side],
            device_id=(me_wide + dx, me_narrow + dy),
            device_id_type=pl.DeviceIdType.MESH,
        )

    started = []

    def send(index, edged, nx, ny, width):
        for side, (dx, dy) in enumerate(SIDES):
            copy = copy_of(index, edged, side, nx, ny, width)
            pl.when(exists(dx, dy))(copy.start)
        started.append((index, edged, nx, ny, width))

    def drain(keep):
        while len(started) > keep:
            index, edged, nx, ny, width = started.pop(0)
            for side, (dx, dy) in enumerate(SIDES):
                copy = copy_of(index, edged, side, nx, ny, width)
                pl.when(exists(dx, dy))(copy.wait_send)

    def receive(index, edged, nx, ny, width):
        drain(2)
        for side, (dx, dy) in enumerate(SIDES):
            copy = copy_of(index, edged, side, nx, ny, width)
            pl.when(exists(-dx, -dy))(copy.wait_recv)

    def put(edged, fields, width):
        rows = fields[0].shape[0]
        for x, field in enumerate(fields):
            edged[x + 1, width : width + rows, :] = field.astype(BF)

    def clear(edged, nx, ny, width):
        lanes = edged.shape[2]
        edged[0] = jnp.zeros(((ny + 2) * width, lanes), BF)
        edged[nx + 1] = jnp.zeros(((ny + 2) * width, lanes), BF)
        for x in range(1, nx + 1):
            edged[x, 0:width, :] = jnp.zeros((width, lanes), BF)
            edged[x, (ny + 1) * width : (ny + 2) * width, :] = jnp.zeros((width, lanes), BF)

    spec_vol = (0, e_vol, xs, ys, c1)
    spec_cot = (1, e_cot, xs, ys, c1)
    spec_p1 = (2, e_p1, x2, y2, c1)
    spec_p2 = (3, e_p2, x3, y3, c2)
    spec_j2 = (4, e_j2, x2, y2, c2)
    spec_j1 = (5, e_j1, xs, ys, c1)
    spec_gd = (6, e_gd, x2, y2, c1)
    spec_gb = (7, e_gb, x3, y3, c3)
    spec_gs = (8, e_gs, x2, y2, c2)
    spec_gf = (9, e_gf, xs, ys, c1)
    for spec in (
        spec_vol, spec_cot, spec_p1, spec_p2, spec_j2, spec_j1, spec_gd, spec_gb, spec_gs, spec_gf
    ):
        clear(*spec[1:])

    barrier = pltpu.get_barrier_semaphore()
    for dx, dy in SIDES:

        @pl.when(exists(dx, dy))
        def _(dx=dx, dy=dy):
            pl.semaphore_signal(
                barrier,
                inc=1,
                device_id=(me_wide + dx, me_narrow + dy),
                device_id_type=pl.DeviceIdType.MESH,
            )

    for load, source, edged in ((loads[0], vol, e_vol), (loads[1], cot, e_cot)):
        load.wait()
        for x in range(xs):
            for y in range(ys):
                edged[x + 1, (y + 1) * c1 : (y + 2) * c1, :] = source[:, x, y, :]
    across = 1 + (me_wide > 0).astype(jnp.int32) + (me_wide < wide_count - 1).astype(jnp.int32)
    along = 1 + (me_narrow > 0).astype(jnp.int32) + (me_narrow < narrow_count - 1).astype(jnp.int32)
    pl.semaphore_wait(barrier, across * along - 1)

    send(*spec_vol)
    send(*spec_cot)

    loads[2].wait()
    turned(w_first, first, ys, c1, c1, False)
    receive(*spec_vol)
    hidden = []
    for x, pre in enumerate(conv(w_first, e_vol, xs, 1)):
        pre_first[x] = pre
        hidden.append(silu(pre).astype(BF))
        hidden_first[x] = hidden[-1]
    pooled = block_sum([h.astype(F32) for h in hidden], c1, 1)
    put(e_p1, [p * 0.125 for p in pooled], c1)
    send(*spec_p1)

    loads[3].wait()
    direct(b_final, final, ys, c1, c1, True)
    receive(*spec_cot)
    joined = [g.astype(BF) for g in conv(b_final, e_cot, xs, 1)]
    for x in range(xs):
        grad_joined[x] = joined[x]
    joined_sum = block_sum([g.astype(F32) for g in joined], c1, 1)

    loads[4].wait()
    turned(w_second, second, y2, c1, c2, False)
    receive(*spec_p1)
    hidden = []
    for x, pre in enumerate(conv(w_second, e_p1, x2, 2)):
        pre_second[x] = pre
        hidden.append(silu(pre).astype(BF))
        hidden_second[x] = hidden[-1]
    pooled = block_sum([h.astype(F32) for h in hidden], c2, 2)
    put(e_p2, [p * 0.125 for p in pooled], c2)
    send(*spec_p2)

    loads[5].wait()
    loads[6].wait()
    turned(w_bottom, bottom, y3, c2, c3, False)
    receive(*spec_p2)
    pre_bottom = conv(w_bottom, e_p2, x3, 4)
    lifted = []
    for pre in pre_bottom:
        hid = silu(pre).astype(BF)
        lifted.append(
            jnp.concatenate(
                [
                    jnp.dot(lift[...], hid[y * c3 : (y + 1) * c3], preferred_element_type=F32)
                    for y in range(y3)
                ],
                axis=0,
            )
        )
    lifted = spread(lifted, c2)
    put(e_j2, [lifted[x] + hidden_second[x].astype(F32) for x in range(x2)], c2)
    send(*spec_j2)

    loads[7].wait()
    direct(w_decode, decode, y2, c1, c2, False)
    receive(*spec_j2)
    pre_decode = conv(w_decode, e_j2, x2, 2)
    put(e_gd, [joined_sum[x] * slope(pre_decode[x]) for x in range(x2)], c1)
    send(*spec_gd)
    decoded = spread([silu(pre).astype(BF).astype(F32) for pre in pre_decode], c1)
    put(e_j1, [decoded[x] + hidden_first[x].astype(F32) for x in range(xs)], c1)
    send(*spec_j1)

    turned(b_decode, decode, y2, c1, c2, True)
    turned(w_final, final, ys, c1, c1, False)
    receive(*spec_gd)
    second_up = [g.astype(BF).astype(F32) for g in conv(b_decode, e_gd, x2, 2)]
    grad_lift = [g.astype(BF) for g in block_sum(second_up, c2, 2)]
    grad_bottom = []
    for x in range(x3):
        back = jnp.concatenate(
            [
                lax.dot_general(
                    lift[...],
                    grad_lift[x][y * c2 : (y + 1) * c2],
                    (((0,), (0,)), ((), ())),
                    preferred_element_type=F32,
                )
                for y in range(y3)
            ],
            axis=0,
        )
        grad_bottom.append(back * slope(pre_bottom[x]))
    put(e_gb, grad_bottom, c3)
    send(*spec_gb)

    receive(*spec_j1)
    for x, out in enumerate(conv(w_final, e_j1, xs, 1)):
        features_ref[x] = out.astype(BF)

    direct(b_bottom, bottom, y3, c2, c3, True)
    receive(*spec_gb)
    pool_second = spread(conv(b_bottom, e_gb, x3, 4), c2)
    put(
        e_gs,
        [(second_up[x] + pool_second[x] * 0.125) * slope(pre_second[x]) for x in range(x2)],
        c2,
    )
    send(*spec_gs)

    direct(b_second, second, y2, c1, c2, True)
    receive(*spec_gs)
    pool_first = spread(conv(b_second, e_gs, x2, 2), c1)
    put(
        e_gf,
        [
            (grad_joined[x].astype(F32) + pool_first[x] * 0.125) * slope(pre_first[x])
            for x in range(xs)
        ],
        c1,
    )
    send(*spec_gf)

    direct(b_first, first, ys, c1, c1, True)
    receive(*spec_gf)
    for x, out in enumerate(conv(b_first, e_gf, xs, 1)):
        grad_ref[x] = out.astype(BF)

    drain(0)


def shards(
    wide_count, narrow_count,
    volume, cotangent, conv_first, conv_second, conv_bottom, lift_weight, conv_decode, conv_final
):
    c1, xs, ys, lanes = volume.shape
    c2, c3 = lift_weight.shape
    x2, y2, x3, y3 = xs // 2, ys // 2, xs // 4, ys // 4

    def back(field):
        return field.reshape(xs, ys, c1, lanes).transpose(2, 0, 1, 3)

    def edged(nx, ny, width):
        return pltpu.VMEM((nx + 2, (ny + 2) * width, lanes), BF)

    def matrix(count, ins, outs):
        return pltpu.VMEM((3 * count * outs, 3 * (count + 2) * ins), BF)

    sizes = ((ys, c1, c1), (y2, c1, c2), (y3, c2, c3), (y2, c2, c1), (ys, c1, c1))
    first, second, bottom, decode, final = (
        k.reshape(27 * k.shape[3], k.shape[4])
        for k in (
            conv_first,
            conv_second,
            conv_bottom,
            conv_decode.transpose(0, 1, 2, 4, 3),
            conv_final,
        )
    )
    shape = jax.ShapeDtypeStruct((xs, ys * c1, lanes), BF)
    vmem = pl.BlockSpec(memory_space=pltpu.VMEM)
    call = pl.pallas_call(
        functools.partial(body, wide_count, narrow_count, xs, ys, (c1, c2, c3)),
        out_shape=(shape, shape),
        in_specs=[pl.BlockSpec(memory_space=pl.ANY)] * 8,
        out_specs=(vmem, vmem),
        scratch_shapes=[
            pltpu.VMEM(volume.shape, BF),
            pltpu.VMEM(cotangent.shape, BF),
            *(pltpu.VMEM(k.shape, BF) for k in (first, second, bottom, lift_weight, decode, final)),
            *(matrix(n, i, o) for n, i, o in sizes),
            *(matrix(n, o, i) for n, i, o in sizes),
            edged(xs, ys, c1),
            edged(xs, ys, c1),
            edged(x2, y2, c1),
            edged(x3, y3, c2),
            edged(x2, y2, c2),
            edged(xs, ys, c1),
            edged(x2, y2, c1),
            edged(x3, y3, c3),
            edged(x2, y2, c2),
            edged(xs, ys, c1),
            pltpu.VMEM((xs, ys * c1, lanes), F32),
            pltpu.VMEM((xs, ys * c1, lanes), BF),
            pltpu.VMEM((xs, ys * c1, lanes), BF),
            pltpu.VMEM((x2, y2 * c2, lanes), F32),
            pltpu.VMEM((x2, y2 * c2, lanes), BF),
            pltpu.SemaphoreType.DMA((10, 8)),
            pltpu.SemaphoreType.DMA((10, 8)),
            pltpu.SemaphoreType.DMA((8,)),
        ],
        compiler_params=pltpu.CompilerParams(
            collective_id=0, has_side_effects=True, vmem_limit_bytes=60 * 1024 * 1024
        ),
    )
    features, grad = call(
        volume, cotangent, first, second, bottom, lift_weight, decode, final
    )
    return back(features), back(grad)


def solution(mesh):
    cells = P(None, "wide", "narrow", None)
    return jax.shard_map(
        functools.partial(shards, mesh.shape["wide"], mesh.shape["narrow"]),
        mesh=mesh,
        in_specs=(cells, cells, P(), P(), P(), P(), P(), P()),
        out_specs=(cells, cells),
        check_vma=False,
    )
```

```python
import functools

import jax
import jax.numpy as jnp
from jax import lax
from jax.experimental import pallas as pl
from jax.experimental.pallas import tpu as pltpu
from jax.sharding import PartitionSpec as P

BF = jnp.bfloat16
F32 = jnp.float32
SIDES = ((-1, -1), (-1, 1), (1, -1), (1, 1), (-1, 0), (1, 0), (0, -1), (0, 1))


def sigmoid(value):
    return jax.nn.sigmoid(value)


def silu(value):
    return value * sigmoid(value)


def slope(value):
    sigma = sigmoid(value)
    return sigma * (1.0 + value * (1.0 - sigma))


def lane_of(value):
    return lax.broadcasted_iota(jnp.int32, value.shape, value.ndim - 1)


def conv(weights, edged, xs, step):
    lanes = edged.shape[2]
    depth = 3 * edged.shape[1]
    rows = weights.shape[0] // 3
    matrix = weights[...]
    outs = []
    parts = []
    for first in range(0, xs, 2):
        group = range(first, min(first + 2, xs))
        wide = jnp.concatenate([edged[x : x + 3].reshape(depth, lanes) for x in group], axis=1)
        both = jnp.dot(matrix, wide, preferred_element_type=F32)
        parts += [both[:, place * lanes : (place + 1) * lanes] for place in range(len(group))]
    for part in parts:
        low, mid, high = part[:rows], part[rows : 2 * rows], part[2 * rows :]
        lane = lane_of(low)
        low = jnp.where(lane < step, 0.0, pltpu.roll(low, step, 1))
        high = jnp.where(lane >= lanes - step, 0.0, pltpu.roll(high, lanes - step, 1))
        outs.append(low + mid + high)
    return outs


def block_sum(fields, chans, step):
    outs = []
    for x in range(0, len(fields), 2):
        both = fields[x] + fields[x + 1]
        rows, lanes = both.shape
        both = jnp.concatenate(
            [
                both[y * chans : (y + 1) * chans] + both[(y + 1) * chans : (y + 2) * chans]
                for y in range(0, rows // chans, 2)
            ],
            axis=0,
        )
        lane = lane_of(both)
        other = jnp.where(
            lax.rem(lane // step, 2) == 0,
            pltpu.roll(both, lanes - step, 1),
            pltpu.roll(both, step, 1),
        )
        outs.append(both + other)
    return outs


def spread(fields, chans):
    outs = []
    for field in fields:
        parts = []
        for y in range(field.shape[0] // chans):
            cell = field[y * chans : (y + 1) * chans]
            parts += [cell, cell]
        wide = jnp.concatenate(parts, axis=0)
        outs += [wide, wide]
    return outs


def tap(kernel, ex, ey, ez, rows, flip):
    if flip:
        ex, ey, ez = 2 - ex, 2 - ey, 2 - ez
    return kernel[pl.ds(((ex * 3 + ey) * 3 + ez) * rows, rows), :]


def turned(out, kernel, ys, rows, columns, flip):
    zero = jnp.zeros((rows, columns), BF)
    strips = [
        jnp.concatenate(
            [
                tap(kernel, ex, rim - y, ez, rows, flip) if 0 <= rim - y < 3 else zero
                for ez in range(3)
                for y in range(ys)
            ],
            axis=1,
        )
        for ex in range(3)
        for rim in range(ys + 2)
    ]
    size = 3 * ys * columns
    row = lax.broadcasted_iota(jnp.int32, (size, size), 0)
    column = lax.broadcasted_iota(jnp.int32, (size, size), 1)
    eye = jnp.where(row == column, 1.0, 0.0).astype(BF)
    out[...] = lax.dot_general(
        eye,
        jnp.concatenate(strips, axis=0),
        (((1,), (1,)), ((), ())),
        preferred_element_type=F32,
    ).astype(BF)


def direct(out, kernel, ys, rows, columns, flip):
    zero = jnp.zeros((rows, columns), BF)
    for ez in range(3):
        for y in range(ys):
            place = (ez * ys + y) * rows
            out[place : place + rows, :] = jnp.concatenate(
                [
                    tap(kernel, ex, rim - y, ez, rows, flip) if 0 <= rim - y < 3 else zero
                    for ex in range(3)
                    for rim in range(ys + 2)
                ],
                axis=1,
            )


def body(
    wide_count, narrow_count, xs, ys, chans,
    vol_in, cot_in, first_in, second_in, bottom_in, lift_in, decode_in, final_in,
    features_ref, grad_ref,
    vol, cot, first, second, bottom, lift, decode, final,
    w_first, w_second, w_bottom, w_decode, w_final,
    b_first, b_second, b_bottom, b_decode, b_final,
    e_vol, e_cot, e_p1, e_p2, e_j2, e_j1, e_gd, e_gb, e_gs, e_gf,
    pre_first, hidden_first, grad_joined, pre_second, hidden_second,
    send_sem, recv_sem, load_sem,
):
    loads = [
        pltpu.make_async_copy(source, target, load_sem.at[place])
        for place, (source, target) in enumerate(
            (
                (vol_in, vol), (cot_in, cot), (first_in, first), (final_in, final),
                (second_in, second), (bottom_in, bottom), (lift_in, lift), (decode_in, decode),
            )
        )
    ]
    for load in loads:
        load.start()
    c1, c2, c3 = chans
    x2, y2 = xs // 2, ys // 2
    x3, y3 = x2 // 2, y2 // 2
    me_wide = lax.axis_index("wide")
    me_narrow = lax.axis_index("narrow")

    def exists(dx, dy):
        near_x, near_y = me_wide + dx, me_narrow + dy
        return (
            (near_x >= 0) & (near_x < wide_count) & (near_y >= 0) & (near_y < narrow_count)
        )

    def span(delta, count, sending):
        if delta == 0:
            return 1, count
        if sending:
            return (count if delta > 0 else 1), 1
        return (0 if delta > 0 else count + 1), 1

    def copy_of(index, edged, side, nx, ny, width):
        dx, dy = SIDES[side]

        def part(sending):
            x_at, x_len = span(dx, nx, sending)
            y_at, y_len = span(dy, ny, sending)
            return edged.at[pl.ds(x_at, x_len), pl.ds(y_at * width, y_len * width), :]

        return pltpu.make_async_remote_copy(
            src_ref=part(True),
            dst_ref=part(False),
            send_sem=send_sem.at[index, side],
            recv_sem=recv_sem.at[index, side],
            device_id=(me_wide + dx, me_narrow + dy),
            device_id_type=pl.DeviceIdType.MESH,
        )

    started = []

    def send(index, edged, nx, ny, width):
        for side, (dx, dy) in enumerate(SIDES):
            copy = copy_of(index, edged, side, nx, ny, width)
            pl.when(exists(dx, dy))(copy.start)
        started.append((index, edged, nx, ny, width))

    def drain(keep):
        while len(started) > keep:
            index, edged, nx, ny, width = started.pop(0)
            for side, (dx, dy) in enumerate(SIDES):
                copy = copy_of(index, edged, side, nx, ny, width)
                pl.when(exists(dx, dy))(copy.wait_send)

    def receive(index, edged, nx, ny, width):
        drain(2)
        for side, (dx, dy) in enumerate(SIDES):
            copy = copy_of(index, edged, side, nx, ny, width)
            pl.when(exists(-dx, -dy))(copy.wait_recv)

    def put(edged, fields, width):
        rows = fields[0].shape[0]
        for x, field in enumerate(fields):
            edged[x + 1, width : width + rows, :] = field.astype(BF)

    def clear(edged, nx, ny, width):
        lanes = edged.shape[2]
        edged[0] = jnp.zeros(((ny + 2) * width, lanes), BF)
        edged[nx + 1] = jnp.zeros(((ny + 2) * width, lanes), BF)
        for x in range(1, nx + 1):
            edged[x, 0:width, :] = jnp.zeros((width, lanes), BF)
            edged[x, (ny + 1) * width : (ny + 2) * width, :] = jnp.zeros((width, lanes), BF)

    spec_vol = (0, e_vol, xs, ys, c1)
    spec_cot = (1, e_cot, xs, ys, c1)
    spec_p1 = (2, e_p1, x2, y2, c1)
    spec_p2 = (3, e_p2, x3, y3, c2)
    spec_j2 = (4, e_j2, x2, y2, c2)
    spec_j1 = (5, e_j1, xs, ys, c1)
    spec_gd = (6, e_gd, x2, y2, c1)
    spec_gb = (7, e_gb, x3, y3, c3)
    spec_gs = (8, e_gs, x2, y2, c2)
    spec_gf = (9, e_gf, xs, ys, c1)
    for spec in (
        spec_vol, spec_cot, spec_p1, spec_p2, spec_j2, spec_j1, spec_gd, spec_gb, spec_gs, spec_gf
    ):
        clear(*spec[1:])

    barrier = pltpu.get_barrier_semaphore()
    for dx, dy in SIDES:

        @pl.when(exists(dx, dy))
        def _(dx=dx, dy=dy):
            pl.semaphore_signal(
                barrier,
                inc=1,
                device_id=(me_wide + dx, me_narrow + dy),
                device_id_type=pl.DeviceIdType.MESH,
            )

    def place_columns(load, source, edged):
        load.wait()
        for x in range(xs):
            for y in range(ys):
                edged[x + 1, (y + 1) * c1 : (y + 2) * c1, :] = source[:, x, y, :]

    place_columns(loads[0], vol, e_vol)
    across = 1 + (me_wide > 0).astype(jnp.int32) + (me_wide < wide_count - 1).astype(jnp.int32)
    along = 1 + (me_narrow > 0).astype(jnp.int32) + (me_narrow < narrow_count - 1).astype(jnp.int32)
    pl.semaphore_wait(barrier, across * along - 1)

    send(*spec_vol)
    place_columns(loads[1], cot, e_cot)
    send(*spec_cot)

    loads[2].wait()
    turned(w_first, first, ys, c1, c1, False)
    receive(*spec_vol)
    hidden = []
    for x, pre in enumerate(conv(w_first, e_vol, xs, 1)):
        pre_first[x] = pre
        hidden.append(silu(pre).astype(BF))
        hidden_first[x] = hidden[-1]
    pooled = block_sum([h.astype(F32) for h in hidden], c1, 1)
    put(e_p1, [p * 0.125 for p in pooled], c1)
    send(*spec_p1)

    loads[3].wait()
    direct(b_final, final, ys, c1, c1, True)
    receive(*spec_cot)
    joined = [g.astype(BF) for g in conv(b_final, e_cot, xs, 1)]
    for x in range(xs):
        grad_joined[x] = joined[x]
    joined_sum = block_sum([g.astype(F32) for g in joined], c1, 1)

    loads[4].wait()
    turned(w_second, second, y2, c1, c2, False)
    receive(*spec_p1)
    hidden = []
    for x, pre in enumerate(conv(w_second, e_p1, x2, 2)):
        pre_second[x] = pre
        hidden.append(silu(pre).astype(BF))
        hidden_second[x] = hidden[-1]
    pooled = block_sum([h.astype(F32) for h in hidden], c2, 2)
    put(e_p2, [p * 0.125 for p in pooled], c2)
    send(*spec_p2)

    loads[5].wait()
    loads[6].wait()
    turned(w_bottom, bottom, y3, c2, c3, False)
    receive(*spec_p2)
    pre_bottom = conv(w_bottom, e_p2, x3, 4)
    lifted = []
    for pre in pre_bottom:
        hid = silu(pre).astype(BF)
        lifted.append(
            jnp.concatenate(
                [
                    jnp.dot(lift[...], hid[y * c3 : (y + 1) * c3], preferred_element_type=F32)
                    for y in range(y3)
                ],
                axis=0,
            )
        )
    lifted = spread(lifted, c2)
    put(e_j2, [lifted[x] + hidden_second[x].astype(F32) for x in range(x2)], c2)
    send(*spec_j2)

    loads[7].wait()
    direct(w_decode, decode, y2, c1, c2, False)
    receive(*spec_j2)
    pre_decode = conv(w_decode, e_j2, x2, 2)
    put(e_gd, [joined_sum[x] * slope(pre_decode[x]) for x in range(x2)], c1)
    send(*spec_gd)
    decoded = spread([silu(pre).astype(BF).astype(F32) for pre in pre_decode], c1)
    put(e_j1, [decoded[x] + hidden_first[x].astype(F32) for x in range(xs)], c1)
    send(*spec_j1)

    turned(b_decode, decode, y2, c1, c2, True)
    turned(w_final, final, ys, c1, c1, False)
    receive(*spec_gd)
    second_up = [g.astype(BF).astype(F32) for g in conv(b_decode, e_gd, x2, 2)]
    grad_lift = [g.astype(BF) for g in block_sum(second_up, c2, 2)]
    grad_bottom = []
    for x in range(x3):
        back = jnp.concatenate(
            [
                lax.dot_general(
                    lift[...],
                    grad_lift[x][y * c2 : (y + 1) * c2],
                    (((0,), (0,)), ((), ())),
                    preferred_element_type=F32,
                )
                for y in range(y3)
            ],
            axis=0,
        )
        grad_bottom.append(back * slope(pre_bottom[x]))
    put(e_gb, grad_bottom, c3)
    send(*spec_gb)

    receive(*spec_j1)
    for x, out in enumerate(conv(w_final, e_j1, xs, 1)):
        features_ref[x] = out.astype(BF)

    direct(b_bottom, bottom, y3, c2, c3, True)
    receive(*spec_gb)
    pool_second = spread(conv(b_bottom, e_gb, x3, 4), c2)
    put(
        e_gs,
        [(second_up[x] + pool_second[x] * 0.125) * slope(pre_second[x]) for x in range(x2)],
        c2,
    )
    send(*spec_gs)

    direct(b_second, second, y2, c1, c2, True)
    receive(*spec_gs)
    pool_first = spread(conv(b_second, e_gs, x2, 2), c1)
    put(
        e_gf,
        [
            (grad_joined[x].astype(F32) + pool_first[x] * 0.125) * slope(pre_first[x])
            for x in range(xs)
        ],
        c1,
    )
    send(*spec_gf)

    direct(b_first, first, ys, c1, c1, True)
    receive(*spec_gf)
    for x, out in enumerate(conv(b_first, e_gf, xs, 1)):
        grad_ref[x] = out.astype(BF)

    drain(0)


def shards(
    wide_count, narrow_count,
    volume, cotangent, conv_first, conv_second, conv_bottom, lift_weight, conv_decode, conv_final
):
    c1, xs, ys, lanes = volume.shape
    c2, c3 = lift_weight.shape
    x2, y2, x3, y3 = xs // 2, ys // 2, xs // 4, ys // 4

    def back(field):
        return field.reshape(xs, ys, c1, lanes).transpose(2, 0, 1, 3)

    def edged(nx, ny, width):
        return pltpu.VMEM((nx + 2, (ny + 2) * width, lanes), BF)

    def matrix(count, ins, outs):
        return pltpu.VMEM((3 * count * outs, 3 * (count + 2) * ins), BF)

    sizes = ((ys, c1, c1), (y2, c1, c2), (y3, c2, c3), (y2, c2, c1), (ys, c1, c1))
    first, second, bottom, decode, final = (
        k.reshape(27 * k.shape[3], k.shape[4])
        for k in (
            conv_first,
            conv_second,
            conv_bottom,
            conv_decode.transpose(0, 1, 2, 4, 3),
            conv_final,
        )
    )
    shape = jax.ShapeDtypeStruct((xs, ys * c1, lanes), BF)
    vmem = pl.BlockSpec(memory_space=pltpu.VMEM)
    call = pl.pallas_call(
        functools.partial(body, wide_count, narrow_count, xs, ys, (c1, c2, c3)),
        out_shape=(shape, shape),
        in_specs=[pl.BlockSpec(memory_space=pl.ANY)] * 8,
        out_specs=(vmem, vmem),
        scratch_shapes=[
            pltpu.VMEM(volume.shape, BF),
            pltpu.VMEM(cotangent.shape, BF),
            *(pltpu.VMEM(k.shape, BF) for k in (first, second, bottom, lift_weight, decode, final)),
            *(matrix(n, i, o) for n, i, o in sizes),
            *(matrix(n, o, i) for n, i, o in sizes),
            edged(xs, ys, c1),
            edged(xs, ys, c1),
            edged(x2, y2, c1),
            edged(x3, y3, c2),
            edged(x2, y2, c2),
            edged(xs, ys, c1),
            edged(x2, y2, c1),
            edged(x3, y3, c3),
            edged(x2, y2, c2),
            edged(xs, ys, c1),
            pltpu.VMEM((xs, ys * c1, lanes), F32),
            pltpu.VMEM((xs, ys * c1, lanes), BF),
            pltpu.VMEM((xs, ys * c1, lanes), BF),
            pltpu.VMEM((x2, y2 * c2, lanes), F32),
            pltpu.VMEM((x2, y2 * c2, lanes), BF),
            pltpu.SemaphoreType.DMA((10, 8)),
            pltpu.SemaphoreType.DMA((10, 8)),
            pltpu.SemaphoreType.DMA((8,)),
        ],
        compiler_params=pltpu.CompilerParams(
            collective_id=0, has_side_effects=True, vmem_limit_bytes=60 * 1024 * 1024
        ),
    )
    features, grad = call(
        volume, cotangent, first, second, bottom, lift_weight, decode, final
    )
    return back(features), back(grad)


def solution(mesh):
    cells = P(None, "wide", "narrow", None)
    return jax.shard_map(
        functools.partial(shards, mesh.shape["wide"], mesh.shape["narrow"]),
        mesh=mesh,
        in_specs=(cells, cells, P(), P(), P(), P(), P(), P()),
        out_specs=(cells, cells),
        check_vma=False,
    )
```
